256 devices in a mesh: band: 8 (over z_hi, core), row: 32 (over y, z_lo, x).
Axes of the slice: x: 4, y: 4, z: 8 (z_hi: 4, z_lo: 2; z = z_hi * 2 + z_lo), core: 2. Of those that a mesh axis runs over, the one named last changes fastest.
Arguments:
- observed: float32 [128, 512, 512], P('band', 'row'), may hold values from -6 to 6
- image: float32 [128, 512, 512], P('band', 'row'), may hold values from -6 to 6
- vector_field: float32 [2, 128, 512, 512], P(None, 'band', 'row'), may hold values from -6 to 6
- dual_grad: float32 [2, 128, 512, 512], P(None, 'band', 'row'), may hold values from -18 to 18
- dual_sym: float32 [3, 128, 512, 512], P(None, 'band', 'row'), may hold values from -18 to 18
- dual_data: float32 [128, 512, 512], P('band', 'row'), may hold values from -6 to 6
- kernels: float32 [16, 15, 15], replicated, may hold values from 0 to 0.03
- kernel_index: int32 [128], P('band'), may hold values from 0 to 15
Outputs:
- image_new: float32 [128, 512, 512], P('band', 'row')
- vector_new: float32 [2, 128, 512, 512], P(None, 'band', 'row')
- grad_new: float32 [2, 128, 512, 512], P(None, 'band', 'row')
- sym_new: float32 [3, 128, 512, 512], P(None, 'band', 'row')
- data_new: float32 [128, 512, 512], P('band', 'row')
The draws below stay inside these ranges and needn't reach their ends.
All inputs are finite; a program needn't handle non-finite values.
Results may differ from the reference program's by a relative error of at most 0.00007.
Values sent between devices are 32-bit elements; how exact they have to be, the bound alone decides.
A program may use at most 128 MiB of HBM per device.

```python
import jax
import jax.numpy as jnp
from jax import lax

BANDS = 128
COLS = 512
KERNEL = 15
NK = 16
ROWS = 512


def dual_values(key, components, spread):
    key_values, key_pixel = jax.random.split(key, 2)
    values = jnp.clip(jax.random.normal(key_values, (components, BANDS, ROWS, COLS), jnp.float32), -4.0, 4.0)
    values = jnp.clip(values, -4.0, 4.0)
    fraction = jnp.arange(BANDS, dtype=jnp.float32) / (BANDS - 1)
    band_scale = 1.5 * spread ** (fraction - 1.0)
    pixel_scale = jnp.exp(jax.random.uniform(key_pixel, (ROWS, COLS), jnp.float32, jnp.log(0.3), jnp.log(3.0)))
    return values * band_scale[None, :, None, None] * pixel_scale


def draw_dual_grad(key, part):
    key = jax.random.fold_in(key, 11)
    return dual_values(key, 2, 3.0)


def draw_dual_sym(key, part):
    key = jax.random.fold_in(key, 12)
    return dual_values(key, 3, 3.0)


def with_ends(values, own_key, smallest, high):
    dims = values.shape
    place = [jax.random.randint(jax.random.fold_in(own_key, axis), (), 0, dims[axis]) for axis in range(len(dims))]
    values = values.at[tuple(place)].set(smallest)
    longest = dims.index(max(dims))
    place[longest] = (place[longest] + 1) % dims[longest]
    return values.at[tuple(place)].set(high)


def block_levels(stream_key, shape, cuts, smallest, top_value):
    def one(position, parts):
        steps = jax.random.uniform(jax.random.fold_in(jax.random.fold_in(stream_key, 6), position), (parts,), jnp.float32, smallest / len(cuts), top_value / len(cuts))
        return jnp.repeat(jnp.exp(steps), shape[position] // parts).reshape((-1,) + (1,) * (len(shape) - position - 1))

    loudness = one(*cuts[0])
    for cut in cuts[1:]:
        loudness = loudness * one(*cut)
    return loudness


def bell_draw(key, shape, width, bound, cuts=(), kind=jnp.bfloat16):
    entries = width * jax.random.normal(key, shape, jnp.float32)
    if cuts:
        entries = entries * block_levels(key, shape, cuts, -0.22, 0.18)
    return jnp.clip(entries, -bound, bound).astype(kind)


def setup_inputs(seed: int = 0) -> dict:
    splits = jax.random.split(jax.random.key(seed), 9)
    observed = bell_draw(splits[0], (BANDS, ROWS, COLS), 1.0, 6.0, ((0, 8), (1, 32)), jnp.float32)
    image = bell_draw(splits[1], (BANDS, ROWS, COLS), 1.0, 6.0, ((0, 8), (1, 32)), jnp.float32)
    vector_field = bell_draw(splits[2], (2, BANDS, ROWS, COLS), 0.5, 6.0, ((1, 8), (2, 32)), jnp.float32)
    dual_grad = draw_dual_grad(jax.random.fold_in(splits[8], 71), 0)
    dual_sym = draw_dual_sym(jax.random.fold_in(splits[8], 71), 0)
    dual_data = bell_draw(splits[5], (BANDS, ROWS, COLS), 1.0, 6.0, ((0, 8), (1, 32)), jnp.float32)
    kernels = jnp.clip(jax.random.uniform(splits[6], (NK, KERNEL, KERNEL), jnp.float32, 0.0, 0.03), 0.0, 0.03)
    kernel_index = with_ends(jax.random.randint(splits[7], (BANDS,), 0, NK), jax.random.fold_in(splits[7], 1), 0, NK - 1).astype(jnp.int32)
    return {"observed": observed, "image": image, "vector_field": vector_field, "dual_grad": dual_grad, "dual_sym": dual_sym, "dual_data": dual_data, "kernels": kernels, "kernel_index": kernel_index}


STEP_PRIMAL = 0.25
STEP_DUAL = 0.25
FIDELITY = 2.0
BOUND_FIRST = 16.0
BOUND_SECOND = 24.0

def blur_full(field, weights):
    radius = KERNEL // 2
    result = lax.conv_general_dilated(field[None], weights[:, None], (1, 1), ((radius, radius), (radius, radius)), dimension_numbers=('NCHW', 'OIHW', 'NCHW'), feature_group_count=field.shape[0], precision=lax.Precision.HIGHEST)
    return result[0]

def row_forward(field):
    following = jnp.concatenate([field[:, 1:], jnp.zeros_like(field[:, :1])], 1)
    return following - field

def row_adjoint(field):
    previous = jnp.concatenate([jnp.zeros_like(field[:, :1]), field[:, :-1]], 1)
    return previous - field

def column_forward(field):
    following = jnp.concatenate([field[:, :, 1:], jnp.zeros_like(field[:, :, :1])], 2)
    return following - field

def column_adjoint(field):
    previous = jnp.concatenate([jnp.zeros_like(field[:, :, :1]), field[:, :, :-1]], 2)
    return previous - field

def reference(observed, image, vector_field, dual_grad, dual_sym, dual_data, kernels, kernel_index):
    weights = kernels[kernel_index]
    flipped = weights[:, ::-1, ::-1]
    image_new = image - STEP_PRIMAL * (blur_full(dual_data, flipped) + row_adjoint(dual_grad[0]) + column_adjoint(dual_grad[1]))
    vector_first = vector_field[0] - STEP_PRIMAL * (row_adjoint(dual_sym[0]) + column_adjoint(dual_sym[2]) - dual_grad[0])
    vector_second = vector_field[1] - STEP_PRIMAL * (column_adjoint(dual_sym[1]) + row_adjoint(dual_sym[2]) - dual_grad[1])
    vector_new = jnp.stack([vector_first, vector_second])
    image_bar = 2.0 * image_new - image
    vector_bar = 2.0 * vector_new - vector_field
    data_new = (dual_data + STEP_DUAL * (blur_full(image_bar, weights) - observed)) / (1.0 + STEP_DUAL / FIDELITY)
    grad_first = dual_grad[0] + STEP_DUAL * (row_forward(image_bar) - vector_bar[0])
    grad_second = dual_grad[1] + STEP_DUAL * (column_forward(image_bar) - vector_bar[1])
    sym_first = dual_sym[0] + STEP_DUAL * row_forward(vector_bar[0])
    sym_second = dual_sym[1] + STEP_DUAL * column_forward(vector_bar[1])
    sym_cross = dual_sym[2] + STEP_DUAL * 0.5 * (column_forward(vector_bar[0]) + row_forward(vector_bar[1]))
    norm_grad = jnp.sqrt(lax.optimization_barrier(jnp.sum(grad_first * grad_first + grad_second * grad_second, axis=0)))
    norm_sym = jnp.sqrt(lax.optimization_barrier(jnp.sum(sym_first * sym_first + sym_second * sym_second + 2.0 * sym_cross * sym_cross, axis=0)))
    scale_grad = 1.0 / jnp.maximum(1.0, norm_grad / BOUND_FIRST)
    scale_sym = 1.0 / jnp.maximum(1.0, norm_sym / BOUND_SECOND)
    grad_new = jnp.stack([grad_first, grad_second]) * scale_grad
    sym_new = jnp.stack([sym_first, sym_second, sym_cross]) * scale_sym
    return (image_new, vector_new, grad_new, sym_new, data_new)
```

```python
import functools

import jax
import jax.numpy as jnp
from jax import lax
from jax.experimental import pallas as pl
from jax.experimental.pallas import tpu as pltpu
from jax.sharding import PartitionSpec as P

FIDELITY = 2.0
STEP_DUAL = 0.25
BOUND_FIRST = 16.0
BOUND_SECOND = 24.0
MESH = pl.DeviceIdType.MESH
F32 = jnp.float32
BF16 = jnp.bfloat16
CHUNK = 4


def split(value):
    high = value.astype(BF16)
    return high, (value - high.astype(F32)).astype(BF16)


def toeplitz_scatter(table_ref, index, out_ref, band):
    lane = lax.broadcasted_iota(jnp.int32, (8, 128), 1)
    first = lane % 32 < 16
    for a in range(4):
        row = jnp.broadcast_to(table_ref[index, pl.ds(a, 1), :], (8, 128))
        groups = []
        for base in (0, 8, -8, 16):
            moved = pltpu.roll(row, (base - 7) % 128, 1, stride=1, stride_axis=0)
            groups.append(jnp.where(first, moved, pltpu.roll(moved, 16, 1)))
        high, low = split(jnp.concatenate(groups, 0))
        out_ref[band, pl.ds(32 * a, 32), pl.ds(0, 128)] = high
        out_ref[band, pl.ds(32 * a, 32), pl.ds(128, 128)] = low


def toeplitz_gather(table_ref, index, out_ref, band):
    lane = lax.broadcasted_iota(jnp.int32, (8, 128), 1) % 32
    for a in range(4):
        row = jnp.broadcast_to(table_ref[index, pl.ds(a, 1), :], (8, 128))
        groups = []
        for base in (0, 8):
            own = pltpu.roll(row, (base - 7) % 128, 1, stride=1, stride_axis=0)
            above = pltpu.roll(row, base + 17, 1, stride=1, stride_axis=0)
            below = pltpu.roll(row, base + 1, 1, stride=1, stride_axis=0)
            groups.append(jnp.where(lane < 16, own, jnp.where(lane < 24, above, below)))
        high, low = split(jnp.concatenate(groups, 0))
        out_ref[band, pl.ds(16 * a, 16), pl.ds(0, 128)] = high
        out_ref[band, pl.ds(16 * a, 16), pl.ds(128, 128)] = high
        out_ref[band, pl.ds(16 * a, 16), pl.ds(256, 128)] = low


def padded_shifts(field):
    rows, cols = field.shape
    wide = jnp.concatenate([field, jnp.zeros((rows, 128), F32)], 1)
    return [split(wide if b == 3 else pltpu.roll(wide, 3 - b, 1)) for b in range(4)]


def gather_shifts(product, rows, cols):
    width = product.shape[1]
    total = product[rows : 2 * rows]
    for a in (0, 2, 3):
        total = total + pltpu.roll(product[a * rows : (a + 1) * rows], (4 - 4 * a) % width, 1)
    return total[:, :cols]


def column_before(field):
    lane = lax.broadcasted_iota(jnp.int32, field.shape, 1)
    return jnp.where(lane == 0, 0.0, pltpu.roll(field, 1, 1))


def column_after(field):
    cols = field.shape[1]
    lane = lax.broadcasted_iota(jnp.int32, field.shape, 1)
    return jnp.where(lane == cols - 1, 0.0, pltpu.roll(field, cols - 1, 1))


def row_before(field, first):
    line = lax.broadcasted_iota(jnp.int32, field.shape, 0)
    return jnp.where(line == 0, first, pltpu.roll(field, 1, 0))


def row_after(field, last):
    rows = field.shape[0]
    line = lax.broadcasted_iota(jnp.int32, field.shape, 0)
    return jnp.where(line == rows - 1, last, pltpu.roll(field, rows - 1, 0))


def kernel(
    bands, rows, cols, band_axis, row_axis,
    index_ref, adjoint_ref, forward_ref,
    observed_hbm, image_hbm, vector_hbm, grad_hbm, sym_hbm, data_hbm,
    image_out, vector_out, grad_out, sym_out, data_out,
    obs, img, vec, grad, sym, data, bar, scatter_w, gather_w,
    line_up, line_dn, line_from_dn, line_from_up,
    near_up, near_dn, near_from_dn, near_from_up,
    far_up, far_dn, far_from_dn, far_from_up,
    part_out, part_in, scale_buf,
    in_sem, out_sem, line_send, line_recv, near_send, near_recv, far_send, far_recv,
    part_send, part_recv, scale_send, scale_recv,
):
    me_row, me_band = lax.axis_index("row"), lax.axis_index("band")
    up = lax.rem(me_row + row_axis - 1, row_axis)
    down = lax.rem(me_row + 1, row_axis)
    peers = [lax.rem(me_band + k, band_axis) for k in range(1, band_axis)]
    not_top = jnp.where(me_row > 0, 1.0, 0.0).astype(F32)
    not_end = jnp.where(me_row < row_axis - 1, 1.0, 0.0).astype(F32)
    chunks = bands // CHUNK

    barrier = pltpu.get_barrier_semaphore()
    for target in (up, down):
        pl.semaphore_signal(barrier, inc=1, device_id={"row": target}, device_id_type=MESH)
    for target in peers:
        pl.semaphore_signal(barrier, inc=1, device_id={"band": target}, device_id_type=MESH)

    loads = [
        pltpu.make_async_copy(source, target, in_sem.at[k])
        for k, (source, target) in enumerate(
            ((sym_hbm, sym), (vector_hbm, vec), (grad_hbm, grad), (data_hbm, data), (image_hbm, img), (observed_hbm, obs))
        )
    ]
    for load in loads:
        load.start()

    def to_row(source, target, send, recv, which):
        return pltpu.make_async_remote_copy(
            src_ref=source, dst_ref=target, send_sem=send, recv_sem=recv,
            device_id={"row": which}, device_id_type=MESH,
        )

    def to_band(source, target, send, recv, which):
        return pltpu.make_async_remote_copy(
            src_ref=source, dst_ref=target, send_sem=send, recv_sem=recv,
            device_id={"band": which}, device_id_type=MESH,
        )

    line_copies = (
        to_row(line_up, line_from_dn, line_send.at[0], line_recv.at[0], up),
        to_row(line_dn, line_from_up, line_send.at[1], line_recv.at[1], down),
    )

    def near_copies(c):
        return (
            to_row(near_up.at[c], near_from_dn.at[c], near_send.at[0, c], near_recv.at[0, c], up),
            to_row(near_dn.at[c], near_from_up.at[c], near_send.at[1, c], near_recv.at[1, c], down),
        )

    def far_copies(c):
        body = pl.ds(8, 6 * CHUNK)
        return (
            to_row(far_up.at[c, body], far_from_dn.at[c, body], far_send.at[0, c], far_recv.at[0, c], up),
            to_row(far_dn.at[c, body], far_from_up.at[c, body], far_send.at[1, c], far_recv.at[1, c], down),
        )

    def scatter_weights(band, carry):
        toeplitz_scatter(adjoint_ref, index_ref[band], scatter_w, band)
        return carry

    lax.fori_loop(0, bands, scatter_weights, 0)

    for load in loads[:3]:
        load.wait()

    def pack_lines(band, carry):
        top = pl.ds(0, 1)
        cross, p0, p1 = sym[2, band, top, :], grad[0, band, top, :], grad[1, band, top, :]
        q0, q1 = sym[0, band, top, :], sym[1, band, top, :]
        line_up[0, band] = vec[0, band, top, :] + 0.5 * (q0 - (column_before(cross) - cross) + p0)
        line_up[1, band] = vec[1, band, top, :] + 0.5 * (cross - (column_before(q1) - q1) + p1)
        line_dn[0, band] = sym[0, band, pl.ds(rows - 1, 1), :]
        line_dn[1, band] = sym[2, band, pl.ds(rows - 1, 1), :]
        return carry

    lax.fori_loop(0, bands, pack_lines, 0)
    pl.semaphore_wait(barrier, 2 + len(peers))
    for copy in line_copies:
        copy.start()

    for load in loads[3:5]:
        load.wait()
    tile_line = lax.broadcasted_iota(jnp.int32, (8, cols), 0)

    def adjoint(c, carry):
        for k in range(CHUNK):
            band = c * CHUNK + k
            parts = [part for pair in padded_shifts(data[band]) for part in pair]
            stacked = jnp.concatenate(parts + parts, 0)
            product = jnp.dot(scatter_w[band], stacked, preferred_element_type=F32)
            total = gather_shifts(product, 2 * rows, cols)
            p0, p1 = grad[0, band], grad[1, band]
            own = img[band] + total[:rows] - 0.5 * (row_before(p0, 0.0) - p0 + column_before(p1) - p1)
            bar[band] = own
            above, below = total[rows : rows + 8], total[rows + 8 : rows + 16]
            near_up[c, k] = jnp.where(tile_line == 0, own[:8], above)
            below = below - jnp.where(tile_line == 0, 0.5 * pltpu.roll(p0[8:], 1, 0), 0.0)
            near_dn[c, k] = jnp.where(tile_line == 7, own[8:], below)
            far_up[c, pl.ds(8 + 6 * k, 6), :] = own[1:7]
            far_dn[c, pl.ds(8 + 6 * k, 6), :] = own[9:15]
        for copy in near_copies(c):
            copy.start()
        return carry

    lax.fori_loop(0, chunks, adjoint, 0)

    def start_far(c, carry):
        for copy in far_copies(c):
            copy.start()
        return carry

    lax.fori_loop(0, chunks, start_far, 0)

    def gather_weights(band, carry):
        toeplitz_gather(forward_ref, index_ref[band], gather_w, band)
        return carry

    lax.fori_loop(0, bands, gather_weights, 0)

    for copy in line_copies:
        copy.wait_recv()

    def symmetric(band, norm):
        q0, q1, q2 = sym[0, band], sym[1, band], sym[2, band]
        p0, p1 = grad[0, band], grad[1, band]
        v0, v1 = vec[0, band], vec[1, band]
        prev0, prev2 = not_top * line_from_up[0, band], not_top * line_from_up[1, band]
        step0 = 0.25 * (row_before(q0, prev0) - q0 + column_before(q2) - q2 - p0)
        step1 = 0.25 * (column_before(q1) - q1 + row_before(q2, prev2) - q2 - p1)
        vec[0, band] = v0 - step0
        vec[1, band] = v1 - step1
        bar0, bar1 = v0 - 2.0 * step0, v1 - 2.0 * step1
        end = pl.ds(rows - 1, 1)
        next0 = not_end * (line_from_dn[0, band] - 0.5 * sym[0, band, end, :])
        next1 = not_end * (line_from_dn[1, band] - 0.5 * sym[2, band, end, :])
        new0 = q0 + 0.25 * (row_after(bar0, next0) - bar0)
        new1 = q1 + 0.25 * (column_after(bar1) - bar1)
        new2 = q2 + 0.125 * (column_after(bar0) - bar0 + row_after(bar1, next1) - bar1)
        sym[0, band] = new0
        sym[1, band] = new1
        sym[2, band] = new2
        grad[0, band] = p0 - 0.25 * bar0
        grad[1, band] = p1 - 0.25 * bar1
        return norm + (new0 * new0 + new1 * new1 + 2.0 * (new2 * new2))

    each = cols // 128 * (rows // 8) // band_axis

    def send_parts(which, norm):
        for piece in range(each * band_axis):
            half, tile = divmod(piece, cols // 128)
            part_out[which, piece // each, piece % each] = norm[8 * half : 8 * half + 8, 128 * tile : 128 * tile + 128]
        part_in[which, me_band] = part_out[which, me_band]
        for peer in peers:
            to_band(
                part_out.at[which, peer], part_in.at[which, me_band],
                part_send.at[which, peer], part_recv.at[which, me_band], peer,
            ).start()

    def send_scales(which, bound):
        for peer in peers:
            to_band(
                part_out.at[which, peer], part_in.at[which, peer],
                part_send.at[which, peer], part_recv.at[which, peer], peer,
            ).wait()
        total = part_in[which, 0]
        for source in range(1, band_axis):
            total = total + part_in[which, source]
        scale_buf[which, me_band] = 1.0 / jnp.maximum(1.0, jnp.sqrt(total) * (1.0 / bound))
        for peer in peers:
            to_band(
                scale_buf.at[which, me_band], scale_buf.at[which, me_band],
                scale_send.at[which, peer], scale_recv.at[which, me_band], peer,
            ).start()

    def wait_scales(which):
        for peer in peers:
            to_band(
                scale_buf.at[which, me_band], scale_buf.at[which, peer],
                scale_send.at[which, peer], scale_recv.at[which, peer], peer,
            ).wait()
        tiles = [scale_buf[which, piece // each, piece % each] for piece in range(each * band_axis)]
        wide = cols // 128
        return jnp.concatenate([jnp.concatenate(tiles[h * wide : h * wide + wide], 1) for h in range(rows // 8)], 0)

    norm_sym = lax.fori_loop(0, bands, symmetric, jnp.zeros((rows, cols), F32))
    send_parts(0, norm_sym)
    store_vec = pltpu.make_async_copy(vec, vector_out, out_sem.at[0])
    store_vec.start()

    def first_order(c, norm):
        for copy in near_copies(c):
            copy.wait_recv()
        for k in range(CHUNK):
            band = c * CHUNK + k
            part = bar[band]
            from_up, from_dn = near_from_up[c, k], near_from_dn[c, k]
            top = part[:8] + jnp.where(tile_line == 7, 0.0, not_top * from_up)
            end = part[8:] + jnp.where(tile_line == 0, 0.0, not_end * from_dn)
            own = jnp.concatenate([top, end], 0)
            bar[band] = own
            img[band] = 0.5 * (img[band] + own)
            following = not_end * (near_from_dn[c, k, pl.ds(0, 1), :] + near_dn[c, k, pl.ds(0, 1), :])
            new0 = grad[0, band] + 0.25 * (row_after(own, following) - own)
            new1 = grad[1, band] + 0.25 * (column_after(own) - own)
            grad[0, band] = new0
            grad[1, band] = new1
            norm = norm + (new0 * new0 + new1 * new1)
        return norm

    norm_grad = lax.fori_loop(0, chunks, first_order, jnp.zeros((rows, cols), F32))
    send_parts(1, norm_grad)
    store_img = pltpu.make_async_copy(img, image_out, out_sem.at[1])
    store_img.start()
    send_scales(0, BOUND_SECOND)
    loads[5].wait()

    def forward(c, carry):
        for copy in far_copies(c):
            copy.wait_recv()
        for k in range(CHUNK):
            band = c * CHUNK + k
            middle = (tile_line >= 1) & (tile_line <= 6)
            near = pl.ds(7 + 6 * k, 8)
            above = jnp.where(middle, far_from_up[c, near, :], near_from_up[c, k])
            above = not_top * jnp.where(tile_line == 0, 0.0, above + near_up[c, k])
            below = jnp.where(middle, far_from_dn[c, near, :], near_from_dn[c, k])
            below = not_end * jnp.where(tile_line == 7, 0.0, below + near_dn[c, k])
            pairs = padded_shifts(jnp.concatenate([bar[band], above, below], 0))
            highs, lows = [pair[0] for pair in pairs], [pair[1] for pair in pairs]
            stacked = jnp.concatenate(highs + lows + highs, 0)
            product = jnp.dot(gather_w[band], stacked, preferred_element_type=F32)
            blurred = gather_shifts(product, rows, cols)
            data[band] = (data[band] + (blurred - STEP_DUAL * obs[band])) * (1.0 / (1.0 + STEP_DUAL / FIDELITY))
        return carry

    lax.fori_loop(0, chunks, forward, 0)
    store_data = pltpu.make_async_copy(data, data_out, out_sem.at[2])
    store_data.start()

    send_scales(1, BOUND_FIRST)
    scale_sym = wait_scales(0)

    def scale_second(band, carry):
        for k in range(3):
            sym[k, band] = sym[k, band] * scale_sym
        return carry

    lax.fori_loop(0, bands, scale_second, 0)
    store_sym = pltpu.make_async_copy(sym, sym_out, out_sem.at[3])
    store_sym.start()

    scale_grad = wait_scales(1)

    def scale_first(band, carry):
        for k in range(2):
            grad[k, band] = grad[k, band] * scale_grad
        return carry

    lax.fori_loop(0, bands, scale_first, 0)
    store_grad = pltpu.make_async_copy(grad, grad_out, out_sem.at[4])
    store_grad.start()

    for copy in line_copies:
        copy.wait_send()

    def finish(c, carry):
        for copy in near_copies(c) + far_copies(c):
            copy.wait_send()
        return carry

    lax.fori_loop(0, chunks, finish, 0)
    for store in (store_vec, store_img, store_data, store_sym, store_grad):
        store.wait()


def spread(kernels, factor):
    count, size, _ = kernels.shape
    turned = jnp.pad(jnp.transpose(kernels, (0, 2, 1)), ((0, 0), (0, 16 - size), (0, 32 - size)))
    return (factor * turned).reshape(count, 4, 128)


def body(band_axis, row_axis, observed, image, vector_field, dual_grad, dual_sym, dual_data, kernels, kernel_index):
    bands, rows, cols = image.shape
    adjoint = spread(kernels[:, ::-1, ::-1], -0.5)
    forward = spread(kernels, STEP_DUAL)
    chunks = bands // CHUNK
    each = cols // 128 * (rows // 8) // band_axis
    vmem = pltpu.VMEM
    near, far = (chunks, CHUNK, 8, cols), (chunks, 16 + 6 * CHUNK, cols)
    line = (2, bands, 1, cols)
    parts = (2, band_axis, each, 8, 128)
    dma = pltpu.SemaphoreType.DMA
    anywhere = pl.BlockSpec(memory_space=pl.ANY)
    inside = pl.BlockSpec(memory_space=pltpu.VMEM)
    arrays = (observed, image, vector_field, dual_grad, dual_sym, dual_data)
    return pl.pallas_call(
        functools.partial(kernel, bands, rows, cols, band_axis, row_axis),
        out_shape=[
            jax.ShapeDtypeStruct(a.shape, F32) for a in (image, vector_field, dual_grad, dual_sym, dual_data)
        ],
        in_specs=[pl.BlockSpec(memory_space=pltpu.SMEM), inside, inside] + [anywhere] * 6,
        out_specs=[anywhere] * 5,
        scratch_shapes=[vmem(a.shape, F32) for a in arrays]
        + [vmem(image.shape, F32), vmem((bands, 8 * rows, 256), BF16), vmem((bands, 4 * rows, 384), BF16)]
        + [vmem(line, F32)] * 4
        + [vmem(near, F32)] * 4
        + [vmem(far, F32)] * 4
        + [vmem(parts, F32)] * 3
        + [dma((6,)), dma((5,)), dma((2,)), dma((2,))]
        + [dma((2, chunks))] * 4
        + [dma((2, band_axis))] * 4,
        compiler_params=pltpu.CompilerParams(
            collective_id=0, has_side_effects=True, vmem_limit_bytes=40 * 1024 * 1024
        ),
    )(kernel_index, adjoint, forward, *arrays)


def solution(mesh):
    placed = (
        P("band", "row", None),
        P("band", "row", None),
        P(None, "band", "row", None),
        P(None, "band", "row", None),
        P(None, "band", "row", None),
        P("band", "row", None),
        P(),
        P("band"),
    )
    return jax.shard_map(
        functools.partial(body, mesh.shape["band"], mesh.shape["row"]),
        mesh=mesh,
        in_specs=placed,
        out_specs=(
            P("band", "row", None),
            P(None, "band", "row", None),
            P(None, "band", "row", None),
            P(None, "band", "row", None),
            P("band", "row", None),
        ),
        check_vma=False,
    )
```

```python
import functools

import jax
import jax.numpy as jnp
from jax import lax
from jax.experimental import pallas as pl
from jax.experimental.pallas import tpu as pltpu
from jax.sharding import PartitionSpec as P

FIDELITY = 2.0
STEP_DUAL = 0.25
BOUND_FIRST = 16.0
BOUND_SECOND = 24.0
MESH = pl.DeviceIdType.MESH
F32 = jnp.float32
BF16 = jnp.bfloat16
CHUNK = 4


def split(value):
    high = value.astype(BF16)
    return high, (value - high.astype(F32)).astype(BF16)


def build_tables(kernels_ref, table_ref):
    size, count, _ = kernels_ref.shape
    groups = []
    for half in range(2):
        total = jnp.zeros((count, 128), F32)
        for i in range(8 * half, min(size, 8 * half + 8)):
            slab = jnp.concatenate([kernels_ref[i], jnp.zeros((count, 128 - size), F32)], 1)
            total = total + (pltpu.roll(slab, 16 * (i % 8), 1) if i % 8 else slab)
        groups.append(total)
    high, low = split(jnp.concatenate(groups, 1))
    values = jnp.concatenate([high, low], 0)
    line = lax.broadcasted_iota(jnp.int32, (256, 128), 0)
    lane = lax.broadcasted_iota(jnp.int32, (256, 128), 1)
    b, i = lane // 32, lane % 32
    for t, factor in enumerate((-0.5, STEP_DUAL)):
        for a in range(4):
            j = 4 * a + b
            place = 16 * (size - 1 - i) + size - 1 - j if t == 0 else 16 * i + j
            place = jnp.where((i < size) & (j < size), place, -1)
            chosen = jnp.where(line == place, 1.0, 0.0).astype(BF16)
            both = jnp.dot(values, chosen, preferred_element_type=F32)
            table_ref[t, a] = factor * (both[:count] + both[count:])


def table_row(table_ref, t, a, index):
    return jnp.broadcast_to(table_ref[t, a, pl.ds(index, 1), :], (8, 128))


def toeplitz_scatter(table_ref, index):
    lane = lax.broadcasted_iota(jnp.int32, (8, 128), 1)
    first = lane % 32 < 16
    groups = []
    for a in range(4):
        row = table_row(table_ref, 0, a, index)
        for base in (0, 8, -8, 16):
            moved = pltpu.roll(row, (base - 7) % 128, 1, stride=1, stride_axis=0)
            groups.append(jnp.where(first, moved, pltpu.roll(moved, 16, 1)))
    return jnp.concatenate(split(jnp.concatenate(groups, 0)), 1)


def toeplitz_gather(table_ref, index):
    lane = lax.broadcasted_iota(jnp.int32, (8, 128), 1) % 32
    groups = []
    for a in range(4):
        row = table_row(table_ref, 1, a, index)
        for base in (0, 8):
            own = pltpu.roll(row, (base - 7) % 128, 1, stride=1, stride_axis=0)
            above = pltpu.roll(row, base + 17, 1, stride=1, stride_axis=0)
            below = pltpu.roll(row, base + 1, 1, stride=1, stride_axis=0)
            groups.append(jnp.where(lane < 16, own, jnp.where(lane < 24, above, below)))
    high, low = split(jnp.concatenate(groups, 0))
    return jnp.concatenate([high, high, low], 1)


def padded_shifts(field):
    rows, cols = field.shape
    wide = jnp.concatenate([field, jnp.zeros((rows, 128), F32)], 1)
    return [split(wide if b == 3 else pltpu.roll(wide, 3 - b, 1)) for b in range(4)]


def gather_shifts(product, rows, cols):
    width = product.shape[1]
    total = product[rows : 2 * rows]
    for a in (0, 2, 3):
        total = total + pltpu.roll(product[a * rows : (a + 1) * rows], (4 - 4 * a) % width, 1)
    return total[:, :cols]


def column_before(field):
    lane = lax.broadcasted_iota(jnp.int32, field.shape, 1)
    return jnp.where(lane == 0, 0.0, pltpu.roll(field, 1, 1))


def column_after(field):
    cols = field.shape[1]
    lane = lax.broadcasted_iota(jnp.int32, field.shape, 1)
    return jnp.where(lane == cols - 1, 0.0, pltpu.roll(field, cols - 1, 1))


def row_before(field, first):
    line = lax.broadcasted_iota(jnp.int32, field.shape, 0)
    return jnp.where(line == 0, first, pltpu.roll(field, 1, 0))


def row_after(field, last):
    rows = field.shape[0]
    line = lax.broadcasted_iota(jnp.int32, field.shape, 0)
    return jnp.where(line == rows - 1, last, pltpu.roll(field, rows - 1, 0))


def kernel(
    bands, rows, cols, band_axis, row_axis,
    index_hbm, kernels_hbm, observed_hbm, image_hbm, vector_hbm, grad_hbm, sym_hbm, data_hbm,
    img, vec, grad, sym, data, scales,
    index_ref, kernels_ref, table, obs, bar, gather_w,
    line_up, line_dn, line_from_dn, line_from_up,
    near_up, near_dn, near_from_dn, near_from_up,
    far_up, far_dn, far_from_dn, far_from_up,
    norms, mate_in, chip_sum, chip_in,
    in_sem, data_sem, line_send, line_recv, near_send, near_recv, far_send, far_recv,
    mate_send, mate_recv, chip_send, chip_recv, back_send, back_recv,
):
    me_row, me_band = lax.axis_index("row"), lax.axis_index("band")
    core, chip = lax.rem(me_band, 2), me_band // 2
    mate = me_band + 1 - 2 * core
    chip_count = band_axis // 2
    peers = [lax.rem(me_band + 2 * k, band_axis) for k in range(1, chip_count)]
    has_up, has_down = me_row > 0, me_row < row_axis - 1
    up, down = me_row - 1, me_row + 1
    not_top = jnp.where(has_up, 1.0, 0.0).astype(F32)
    not_end = jnp.where(has_down, 1.0, 0.0).astype(F32)
    chunks = bands // CHUNK

    barrier = pltpu.get_barrier_semaphore()

    def greet(**target):
        pl.semaphore_signal(barrier, inc=1, device_id=target, device_id_type=MESH)

    pl.when(has_up)(lambda: greet(row=up))
    pl.when(has_down)(lambda: greet(row=down))
    greet(band=mate)
    for peer in peers:
        greet(band=peer)

    def fetch(source, target, sem):
        copy = pltpu.make_async_copy(source, target, sem)
        copy.start()
        return copy

    load_index = fetch(index_hbm, index_ref, in_sem.at[0])
    load_kernels = fetch(kernels_hbm, kernels_ref, in_sem.at[1])
    load_sym = fetch(sym_hbm, sym, in_sem.at[2])
    load_grad = fetch(grad_hbm, grad, in_sem.at[3])
    load_vec = fetch(vector_hbm, vec, in_sem.at[4])
    load_data = fetch(data_hbm, data, in_sem.at[5])
    load_img = fetch(image_hbm, img, in_sem.at[6])
    load_obs = fetch(observed_hbm, obs, in_sem.at[7])

    def remote(source, target, send, recv, **which):
        return pltpu.make_async_remote_copy(
            src_ref=source, dst_ref=target, send_sem=send, recv_sem=recv,
            device_id=which, device_id_type=MESH,
        )

    def line_copies():
        return (
            remote(line_up, line_from_dn, line_send.at[0], line_recv.at[0], row=up),
            remote(line_dn, line_from_up, line_send.at[1], line_recv.at[1], row=down),
        )

    def near_copies(c):
        return (
            remote(near_up.at[c], near_from_dn.at[c], near_send.at[0, c], near_recv.at[0, c], row=up),
            remote(near_dn.at[c], near_from_up.at[c], near_send.at[1, c], near_recv.at[1, c], row=down),
        )

    def far_copies(c):
        body = pl.ds(8, 6 * CHUNK)
        return (
            remote(far_up.at[c, body], far_from_dn.at[c, body], far_send.at[0, c], far_recv.at[0, c], row=up),
            remote(far_dn.at[c, body], far_from_up.at[c, body], far_send.at[1, c], far_recv.at[1, c], row=down),
        )

    def start(copies):
        pl.when(has_up)(copies[0].start)
        pl.when(has_down)(copies[1].start)

    def wait_recv(copies):
        pl.when(has_down)(copies[0].wait_recv)
        pl.when(has_up)(copies[1].wait_recv)

    def wait_send(copies):
        pl.when(has_up)(copies[0].wait_send)
        pl.when(has_down)(copies[1].wait_send)

    @pl.when(jnp.logical_not(has_up))
    def _():
        for ref in (line_from_up, near_from_up, far_from_up):
            ref[...] = jnp.zeros(ref.shape, F32)

    @pl.when(jnp.logical_not(has_down))
    def _():
        for ref in (line_from_dn, near_from_dn, far_from_dn):
            ref[...] = jnp.zeros(ref.shape, F32)

    load_kernels.wait()
    build_tables(kernels_ref, table)

    load_sym.wait()
    load_grad.wait()
    load_vec.wait()

    def pack_lines(c, carry):
        for k in range(CHUNK):
            band = c * CHUNK + k
            top = pl.ds(0, 1)
            cross, p0, p1 = sym[2, band, top, :], grad[0, band, top, :], grad[1, band, top, :]
            q0, q1 = sym[0, band, top, :], sym[1, band, top, :]
            line_up[0, band] = vec[0, band, top, :] + 0.5 * (q0 - (column_before(cross) - cross) + p0)
            line_up[1, band] = vec[1, band, top, :] + 0.5 * (cross - (column_before(q1) - q1) + p1)
            line_dn[0, band] = sym[0, band, pl.ds(rows - 1, 1), :]
            line_dn[1, band] = sym[2, band, pl.ds(rows - 1, 1), :]
        return carry

    lax.fori_loop(0, chunks, pack_lines, 0)
    pl.semaphore_wait(barrier, 1 + len(peers) + has_up.astype(jnp.int32) + has_down.astype(jnp.int32))
    start(line_copies())

    load_index.wait()
    load_data.wait()
    load_img.wait()
    tile_line = lax.broadcasted_iota(jnp.int32, (8, cols), 0)

    def adjoint(c, carry):
        for k in range(CHUNK):
            band = c * CHUNK + k
            parts = [part for pair in padded_shifts(data[band]) for part in pair]
            stacked = jnp.concatenate(parts + parts, 0)
            weights = toeplitz_scatter(table, index_ref[band])
            product = jnp.dot(weights, stacked, preferred_element_type=F32)
            total = gather_shifts(product, 2 * rows, cols)
            p0, p1 = grad[0, band], grad[1, band]
            own = img[band] + total[:rows] - 0.5 * (row_before(p0, 0.0) - p0 + column_before(p1) - p1)
            bar[band] = own
            above, below = total[rows : rows + 8], total[rows + 8 : rows + 16]
            near_up[c, k] = jnp.where(tile_line == 0, own[:8], above)
            below = below - jnp.where(tile_line == 0, 0.5 * pltpu.roll(p0[8:], 1, 0), 0.0)
            near_dn[c, k] = jnp.where(tile_line == 7, own[8:], below)
            far_up[c, pl.ds(8 + 6 * k, 6), :] = own[1:7]
            far_dn[c, pl.ds(8 + 6 * k, 6), :] = own[9:15]
        start(near_copies(c))
        return carry

    lax.fori_loop(0, chunks, adjoint, 0)

    def start_far(c, carry):
        start(far_copies(c))
        return carry

    lax.fori_loop(0, chunks, start_far, 0)

    wait_recv(line_copies())

    def symmetric(step, norm):
        for k in range(2):
            band = 2 * step + k
            q0, q1, q2 = sym[0, band], sym[1, band], sym[2, band]
            p0, p1 = grad[0, band], grad[1, band]
            v0, v1 = vec[0, band], vec[1, band]
            prev0, prev2 = not_top * line_from_up[0, band], not_top * line_from_up[1, band]
            step0 = 0.25 * (row_before(q0, prev0) - q0 + column_before(q2) - q2 - p0)
            step1 = 0.25 * (column_before(q1) - q1 + row_before(q2, prev2) - q2 - p1)
            vec[0, band] = v0 - step0
            vec[1, band] = v1 - step1
            bar0, bar1 = v0 - 2.0 * step0, v1 - 2.0 * step1
            end = pl.ds(rows - 1, 1)
            next0 = not_end * (line_from_dn[0, band] - 0.5 * sym[0, band, end, :])
            next1 = not_end * (line_from_dn[1, band] - 0.5 * sym[2, band, end, :])
            new0 = q0 + 0.25 * (row_after(bar0, next0) - bar0)
            new1 = q1 + 0.25 * (column_after(bar1) - bar1)
            new2 = q2 + 0.125 * (column_after(bar0) - bar0 + row_after(bar1, next1) - bar1)
            sym[0, band] = new0
            sym[1, band] = new1
            sym[2, band] = new2
            grad[0, band] = p0 - 0.25 * bar0
            grad[1, band] = p1 - 0.25 * bar1
            norm = norm + (new0 * new0 + new1 * new1 + 2.0 * (new2 * new2))
        return norm

    def mate_copy(which):
        return remote(norms.at[which, 1 - core], mate_in.at[which], mate_send.at[which], mate_recv.at[which], band=mate)

    def chip_copy(which, peer, slot):
        return remote(
            chip_sum.at[which], chip_in.at[which, slot],
            chip_send.at[which, peer // 2], chip_recv.at[which, slot], band=peer,
        )

    def back_copy(which, half):
        return remote(scales.at[which, core], scales.at[which, half], back_send.at[which], back_recv.at[which], band=mate)

    def send_norm(which, norm):
        norms[which, 0] = norm[:8]
        norms[which, 1] = norm[8:]
        mate_copy(which).start()

    def send_chip(which):
        mate_copy(which).wait()
        total = norms[which, core] + mate_in[which]
        chip_sum[which] = total
        chip_in[which, chip] = total
        for peer in peers:
            chip_copy(which, peer, chip).start()

    def send_scale(which, bound):
        for peer in peers:
            chip_copy(which, peer, peer // 2).wait()
        total = chip_in[which, 0]
        for other in range(1, chip_count):
            total = total + chip_in[which, other]
        scales[which, core] = 1.0 / jnp.maximum(1.0, jnp.sqrt(total) * (1.0 / bound))
        back_copy(which, core).start()

    norm_sym = lax.fori_loop(0, bands // 2, symmetric, jnp.zeros((rows, cols), F32))
    send_norm(0, norm_sym)

    def gather_weights(band, carry):
        gather_w[band] = toeplitz_gather(table, index_ref[band])
        return carry

    lax.fori_loop(0, bands, gather_weights, 0)
    send_chip(0)

    def first_order(c, norm):
        wait_recv(near_copies(c))
        for k in range(CHUNK):
            band = c * CHUNK + k
            part = bar[band]
            from_up, from_dn = near_from_up[c, k], near_from_dn[c, k]
            top = part[:8] + jnp.where(tile_line == 7, 0.0, not_top * from_up)
            end = part[8:] + jnp.where(tile_line == 0, 0.0, not_end * from_dn)
            own = jnp.concatenate([top, end], 0)
            bar[band] = own
            img[band] = 0.5 * (img[band] + own)
            following = not_end * (near_from_dn[c, k, pl.ds(0, 1), :] + near_dn[c, k, pl.ds(0, 1), :])
            new0 = grad[0, band] + 0.25 * (row_after(own, following) - own)
            new1 = grad[1, band] + 0.25 * (column_after(own) - own)
            grad[0, band] = new0
            grad[1, band] = new1
            norm = norm + (new0 * new0 + new1 * new1)
        return norm

    norm_grad = lax.fori_loop(0, chunks, first_order, jnp.zeros((rows, cols), F32))
    send_norm(1, norm_grad)
    load_obs.wait()
    send_chip(1)

    def forward(c, carry):
        wait_recv(far_copies(c))
        for k in range(CHUNK):
            band = c * CHUNK + k
            middle = (tile_line >= 1) & (tile_line <= 6)
            near = pl.ds(7 + 6 * k, 8)
            above = jnp.where(middle, far_from_up[c, near, :], near_from_up[c, k])
            above = not_top * jnp.where(tile_line == 0, 0.0, above + near_up[c, k])
            below = jnp.where(middle, far_from_dn[c, near, :], near_from_dn[c, k])
            below = not_end * jnp.where(tile_line == 7, 0.0, below + near_dn[c, k])
            pairs = padded_shifts(jnp.concatenate([bar[band], above, below], 0))
            highs, lows = [pair[0] for pair in pairs], [pair[1] for pair in pairs]
            stacked = jnp.concatenate(highs + lows + highs, 0)
            product = jnp.dot(gather_w[band], stacked, preferred_element_type=F32)
            blurred = gather_shifts(product, rows, cols)
            data[band] = (data[band] + (blurred - STEP_DUAL * obs[band])) * (1.0 / (1.0 + STEP_DUAL / FIDELITY))
        return carry

    lax.fori_loop(0, chunks, forward, 0)
    send_scale(0, BOUND_SECOND)
    send_scale(1, BOUND_FIRST)

    wait_send(line_copies())

    def finish(c, carry):
        wait_send(near_copies(c))
        wait_send(far_copies(c))
        return carry

    lax.fori_loop(0, chunks, finish, 0)
    for which in range(2):
        back_copy(which, 1 - core).wait()


def finish_kernel(
    img, vec, grad, sym, data, scales,
    image_out, vector_out, grad_out, sym_out, data_out,
    scaled_sym, scaled_grad, plain_sem, sym_sem, grad_sem,
):
    plain = [
        pltpu.make_async_copy(source, target, plain_sem.at[k])
        for k, (source, target) in enumerate(((vec, vector_out), (img, image_out), (data, data_out)))
    ]
    for copy in plain:
        copy.start()
    chunks = img.shape[0] // CHUNK
    factor_sym = jnp.concatenate([scales[0, 0], scales[0, 1]], 0)
    factor_grad = jnp.concatenate([scales[1, 0], scales[1, 1]], 0)

    def stores(c):
        part = pl.ds(c * CHUNK, CHUNK)
        return (
            pltpu.make_async_copy(scaled_sym.at[:, part], sym_out.at[:, part], sym_sem.at[c]),
            pltpu.make_async_copy(scaled_grad.at[:, part], grad_out.at[:, part], grad_sem.at[c]),
        )

    def scale(c, carry):
        for k in range(CHUNK):
            band = c * CHUNK + k
            for part in range(3):
                scaled_sym[part, band] = sym[part, band] * factor_sym
            for part in range(2):
                scaled_grad[part, band] = grad[part, band] * factor_grad
        for copy in stores(c):
            copy.start()
        return carry

    lax.fori_loop(0, chunks, scale, 0)

    def wait(c, carry):
        for copy in stores(c):
            copy.wait()
        return carry

    lax.fori_loop(0, chunks, wait, 0)
    for copy in plain:
        copy.wait()


def body(band_axis, row_axis, observed, image, vector_field, dual_grad, dual_sym, dual_data, kernels, kernel_index):
    bands, rows, cols = image.shape
    chunks = bands // CHUNK
    turned = jnp.transpose(kernels, (1, 0, 2))
    size, count, _ = turned.shape
    vmem, hbm, dma = pltpu.VMEM, pltpu.HBM, pltpu.SemaphoreType.DMA
    near, far = (chunks, CHUNK, 8, cols), (chunks, 16 + 6 * CHUNK, cols)
    line, half = (2, bands, 1, cols), (8, cols)
    anywhere = pl.BlockSpec(memory_space=pl.ANY)
    inside = pl.BlockSpec(memory_space=pltpu.VMEM)
    results = (image, vector_field, dual_grad, dual_sym, dual_data)
    inputs = (kernel_index, turned, observed, image, vector_field, dual_grad, dual_sym, dual_data)
    held = pl.pallas_call(
        functools.partial(kernel, bands, rows, cols, band_axis, row_axis),
        out_shape=[vmem(a.shape, F32) for a in results] + [vmem((2, 2, *half), F32)],
        in_specs=[anywhere] * 8,
        out_specs=[inside] * 6,
        scratch_shapes=[
            pltpu.SMEM(kernel_index.shape, jnp.int32),
            vmem((size, count, size), F32),
            vmem((2, 4, count, 128), F32),
            vmem(image.shape, F32),
            vmem(image.shape, F32),
            vmem((bands, 4 * rows, 384), BF16),
        ]
        + [vmem(line, F32)] * 4
        + [vmem(near, F32)] * 4
        + [vmem(far, F32)] * 4
        + [vmem((2, 2, *half), F32), vmem((2, *half), F32), vmem((2, *half), F32), vmem((2, band_axis // 2, *half), F32)]
        + [dma((8,)), dma((1,)), dma((2,)), dma((2,))]
        + [dma((2, chunks))] * 4
        + [dma((2,))] * 2
        + [dma((2, band_axis // 2))] * 2
        + [dma((2,))] * 2,
        compiler_params=pltpu.CompilerParams(
            collective_id=0, has_side_effects=True, vmem_limit_bytes=24 * 1024 * 1024
        ),
    )(*[pltpu.with_memory_space_constraint(a, hbm) for a in inputs])
    return pl.pallas_call(
        finish_kernel,
        out_shape=[hbm(a.shape, F32) for a in results],
        in_specs=[inside] * 6,
        out_specs=[anywhere] * 5,
        scratch_shapes=[vmem(dual_sym.shape, F32), vmem(dual_grad.shape, F32), dma((3,)), dma((chunks,)), dma((chunks,))],
        compiler_params=pltpu.CompilerParams(vmem_limit_bytes=16 * 1024 * 1024),
    )(*[pltpu.with_memory_space_constraint(a, vmem) for a in held])


def solution(mesh):
    placed = (
        P("band", "row", None),
        P("band", "row", None),
        P(None, "band", "row", None),
        P(None, "band", "row", None),
        P(None, "band", "row", None),
        P("band", "row", None),
        P(),
        P("band"),
    )
    return jax.shard_map(
        functools.partial(body, mesh.shape["band"], mesh.shape["row"]),
        mesh=mesh,
        in_specs=placed,
        out_specs=(
            P("band", "row", None),
            P(None, "band", "row", None),
            P(None, "band", "row", None),
            P(None, "band", "row", None),
            P("band", "row", None),
        ),
        check_vma=False,
    )
```

```python
import functools

import jax
import jax.numpy as jnp
from jax import lax
from jax.experimental import pallas as pl
from jax.experimental.pallas import tpu as pltpu
from jax.sharding import PartitionSpec as P

FIDELITY = 2.0
STEP_DUAL = 0.25
BOUND_FIRST = 16.0
BOUND_SECOND = 24.0
MESH = pl.DeviceIdType.MESH
F32 = jnp.float32
BF16 = jnp.bfloat16
CHUNK = 4


def split(value):
    high = value.astype(BF16)
    return high, (value - high.astype(F32)).astype(BF16)


def build_tables(kernels_ref, table_ref):
    size, count, _ = kernels_ref.shape
    groups = []
    for half in range(2):
        total = jnp.zeros((count, 128), F32)
        for i in range(8 * half, min(size, 8 * half + 8)):
            slab = jnp.concatenate([kernels_ref[i], jnp.zeros((count, 128 - size), F32)], 1)
            total = total + (pltpu.roll(slab, 16 * (i % 8), 1) if i % 8 else slab)
        groups.append(total)
    high, low = split(jnp.concatenate(groups, 1))
    values = jnp.concatenate([high, low], 0)
    line = lax.broadcasted_iota(jnp.int32, (256, 128), 0)
    lane = lax.broadcasted_iota(jnp.int32, (256, 128), 1)
    b, i = lane // 32, lane % 32
    for t, factor in enumerate((-0.5, STEP_DUAL)):
        for a in range(4):
            j = 4 * a + b
            place = 16 * (size - 1 - i) + size - 1 - j if t == 0 else 16 * i + j
            place = jnp.where((i < size) & (j < size), place, -1)
            chosen = jnp.where(line == place, 1.0, 0.0).astype(BF16)
            both = jnp.dot(values, chosen, preferred_element_type=F32)
            table_ref[t, a] = factor * (both[:count] + both[count:])


def table_row(table_ref, t, a, index):
    return jnp.broadcast_to(table_ref[t, a, pl.ds(index, 1), :], (8, 128))


def toeplitz_scatter(table_ref, index):
    lane = lax.broadcasted_iota(jnp.int32, (8, 128), 1)
    first = lane % 32 < 16
    groups = []
    for a in range(4):
        row = table_row(table_ref, 0, a, index)
        for base in (0, 8, -8, 16):
            moved = pltpu.roll(row, (base - 7) % 128, 1, stride=1, stride_axis=0)
            groups.append(jnp.where(first, moved, pltpu.roll(moved, 16, 1)))
    return jnp.concatenate(split(jnp.concatenate(groups, 0)), 1)


def toeplitz_gather(table_ref, index):
    lane = lax.broadcasted_iota(jnp.int32, (8, 128), 1) % 32
    groups = []
    for a in range(4):
        row = table_row(table_ref, 1, a, index)
        for base in (0, 8):
            own = pltpu.roll(row, (base - 7) % 128, 1, stride=1, stride_axis=0)
            above = pltpu.roll(row, base + 17, 1, stride=1, stride_axis=0)
            below = pltpu.roll(row, base + 1, 1, stride=1, stride_axis=0)
            groups.append(jnp.where(lane < 16, own, jnp.where(lane < 24, above, below)))
    high, low = split(jnp.concatenate(groups, 0))
    return jnp.concatenate([high, high, low], 1)


def padded_shifts(field):
    rows, cols = field.shape
    wide = jnp.concatenate([field, jnp.zeros((rows, 128), F32)], 1)
    return [split(wide if b == 3 else pltpu.roll(wide, 3 - b, 1)) for b in range(4)]


def gather_shifts(product, rows, cols):
    width = product.shape[1]
    total = product[rows : 2 * rows]
    for a in (0, 2, 3):
        total = total + pltpu.roll(product[a * rows : (a + 1) * rows], (4 - 4 * a) % width, 1)
    return total[:, :cols]


def column_before(field):
    lane = lax.broadcasted_iota(jnp.int32, field.shape, 1)
    return jnp.where(lane == 0, 0.0, pltpu.roll(field, 1, 1))


def column_after(field):
    cols = field.shape[1]
    lane = lax.broadcasted_iota(jnp.int32, field.shape, 1)
    return jnp.where(lane == cols - 1, 0.0, pltpu.roll(field, cols - 1, 1))


def row_before(field, first):
    line = lax.broadcasted_iota(jnp.int32, field.shape, 0)
    return jnp.where(line == 0, first, pltpu.roll(field, 1, 0))


def row_after(field, last):
    rows = field.shape[0]
    line = lax.broadcasted_iota(jnp.int32, field.shape, 0)
    return jnp.where(line == rows - 1, last, pltpu.roll(field, rows - 1, 0))


def kernel(
    bands, rows, cols, band_axis, row_axis,
    index_hbm, kernels_hbm, observed_hbm, image_hbm, vector_hbm, grad_hbm, sym_hbm, data_hbm,
    img, vec, grad, sym, data, scales,
    index_ref, kernels_ref, table, obs, bar, gather_w,
    line_up, line_dn, line_from_dn, line_from_up,
    near_up, near_dn, near_from_dn, near_from_up,
    far_up, far_dn, far_from_dn, far_from_up,
    norms, mate_in, chip_sum, chip_in,
    in_sem, data_sem, line_send, line_recv, near_send, near_recv, far_send, far_recv,
    mate_send, mate_recv, chip_send, chip_recv, back_send, back_recv, ready,
):
    me_row, me_band = lax.axis_index("row"), lax.axis_index("band")
    core, chip = lax.rem(me_band, 2), me_band // 2
    mate = me_band + 1 - 2 * core
    chip_count = band_axis // 2
    peers = [lax.rem(me_band + 2 * k, band_axis) for k in range(1, chip_count)]
    has_up, has_down = me_row > 0, me_row < row_axis - 1
    up, down = me_row - 1, me_row + 1
    not_top = jnp.where(has_up, 1.0, 0.0).astype(F32)
    not_end = jnp.where(has_down, 1.0, 0.0).astype(F32)
    chunks = bands // CHUNK

    barrier = pltpu.get_barrier_semaphore()

    def greet(**target):
        pl.semaphore_signal(barrier, inc=1, device_id=target, device_id_type=MESH)

    pl.when(has_up)(lambda: greet(row=up))
    pl.when(has_down)(lambda: greet(row=down))
    greet(band=mate)
    for peer in peers:
        pl.when(peer > me_band)(functools.partial(greet, band=peer))

    def fetch(source, target, sem):
        copy = pltpu.make_async_copy(source, target, sem)
        copy.start()
        return copy

    load_index = fetch(index_hbm, index_ref, in_sem.at[0])
    load_kernels = fetch(kernels_hbm, kernels_ref, in_sem.at[1])
    load_sym = fetch(sym_hbm, sym, in_sem.at[2])
    load_grad = fetch(grad_hbm, grad, in_sem.at[3])
    load_vec = fetch(vector_hbm, vec, in_sem.at[4])
    load_data = fetch(data_hbm, data, in_sem.at[5])
    load_img = fetch(image_hbm, img, in_sem.at[6])
    load_obs = fetch(observed_hbm, obs, in_sem.at[7])

    def remote(source, target, send, recv, **which):
        return pltpu.make_async_remote_copy(
            src_ref=source, dst_ref=target, send_sem=send, recv_sem=recv,
            device_id=which, device_id_type=MESH,
        )

    def line_copies():
        return (
            remote(line_up, line_from_dn, line_send.at[0], line_recv.at[0], row=up),
            remote(line_dn, line_from_up, line_send.at[1], line_recv.at[1], row=down),
        )

    def near_copies(c):
        return (
            remote(near_up.at[c], near_from_dn.at[c], near_send.at[0, c], near_recv.at[0, c], row=up),
            remote(near_dn.at[c], near_from_up.at[c], near_send.at[1, c], near_recv.at[1, c], row=down),
        )

    def far_copies(c):
        body = pl.ds(8, 6 * CHUNK)
        return (
            remote(far_up.at[c, body], far_from_dn.at[c, body], far_send.at[0, c], far_recv.at[0, c], row=up),
            remote(far_dn.at[c, body], far_from_up.at[c, body], far_send.at[1, c], far_recv.at[1, c], row=down),
        )

    def start(copies):
        pl.when(has_up)(copies[0].start)
        pl.when(has_down)(copies[1].start)

    def wait_recv(copies):
        pl.when(has_down)(copies[0].wait_recv)
        pl.when(has_up)(copies[1].wait_recv)

    def wait_send(copies):
        pl.when(has_up)(copies[0].wait_send)
        pl.when(has_down)(copies[1].wait_send)

    @pl.when(jnp.logical_not(has_up))
    def _():
        for ref in (line_from_up, near_from_up, far_from_up):
            ref[...] = jnp.zeros(ref.shape, F32)

    @pl.when(jnp.logical_not(has_down))
    def _():
        for ref in (line_from_dn, near_from_dn, far_from_dn):
            ref[...] = jnp.zeros(ref.shape, F32)

    load_kernels.wait()
    build_tables(kernels_ref, table)

    load_sym.wait()
    load_grad.wait()
    load_vec.wait()

    def lines_of(ref, part, row):
        return ref[part, :, row, :]

    q0, q1, cross = [lines_of(sym, part, 0) for part in range(3)]
    line_up[0] = lines_of(vec, 0, 0) + 0.5 * (q0 - (column_before(cross) - cross) + lines_of(grad, 0, 0))
    line_up[1] = lines_of(vec, 1, 0) + 0.5 * (cross - (column_before(q1) - q1) + lines_of(grad, 1, 0))
    line_dn[0] = lines_of(sym, 0, rows - 1)
    line_dn[1] = lines_of(sym, 2, rows - 1)
    pl.semaphore_wait(barrier, 1 + chip + has_up.astype(jnp.int32) + has_down.astype(jnp.int32))

    def answer(peer):
        pl.semaphore_signal(ready, inc=1, device_id={"band": peer}, device_id_type=MESH)

    for peer in peers:
        pl.when(peer < me_band)(functools.partial(answer, peer))
    start(line_copies())

    load_index.wait()
    load_data.wait()
    load_img.wait()
    tile_line = lax.broadcasted_iota(jnp.int32, (8, cols), 0)

    def adjoint(c, carry):
        for k in range(CHUNK):
            band = c * CHUNK + k
            parts = [part for pair in padded_shifts(data[band]) for part in pair]
            stacked = jnp.concatenate(parts + parts, 0)
            weights = toeplitz_scatter(table, index_ref[band])
            product = jnp.dot(weights, stacked, preferred_element_type=F32)
            total = gather_shifts(product, 2 * rows, cols)
            p0, p1 = grad[0, band], grad[1, band]
            own = img[band] + total[:rows] - 0.5 * (row_before(p0, 0.0) - p0 + column_before(p1) - p1)
            bar[band] = own
            above, below = total[rows : rows + 8], total[rows + 8 : rows + 16]
            near_up[c, k] = jnp.where(tile_line == 0, own[:8], above)
            below = below - jnp.where(tile_line == 0, 0.5 * pltpu.roll(p0[8:], 1, 0), 0.0)
            near_dn[c, k] = jnp.where(tile_line == 7, own[8:], below)
            far_up[c, pl.ds(8 + 6 * k, 6), :] = own[1:7]
            far_dn[c, pl.ds(8 + 6 * k, 6), :] = own[9:15]
        start(near_copies(c))
        return carry

    lax.fori_loop(0, chunks, adjoint, 0)

    def start_far(c, carry):
        start(far_copies(c))


    pl.when(chip < chip_count // 2)(lambda: lax.fori_loop(0, chunks, start_far, None))

    wait_recv(line_copies())

    def symmetric(step, norm):
        for k in range(2):
            band = 2 * step + k
            q0, q1, q2 = sym[0, band], sym[1, band], sym[2, band]
            p0, p1 = grad[0, band], grad[1, band]
            v0, v1 = vec[0, band], vec[1, band]
            here = pl.ds(band, 1)
            prev0, prev2 = not_top * line_from_up[0, here, :], not_top * line_from_up[1, here, :]
            step0 = 0.25 * (row_before(q0, prev0) - q0 + column_before(q2) - q2 - p0)
            step1 = 0.25 * (column_before(q1) - q1 + row_before(q2, prev2) - q2 - p1)
            vec[0, band] = v0 - step0
            vec[1, band] = v1 - step1
            bar0, bar1 = v0 - 2.0 * step0, v1 - 2.0 * step1
            end = pl.ds(rows - 1, 1)
            next0 = not_end * (line_from_dn[0, here, :] - 0.5 * sym[0, band, end, :])
            next1 = not_end * (line_from_dn[1, here, :] - 0.5 * sym[2, band, end, :])
            new0 = q0 + 0.25 * (row_after(bar0, next0) - bar0)
            new1 = q1 + 0.25 * (column_after(bar1) - bar1)
            new2 = q2 + 0.125 * (column_after(bar0) - bar0 + row_after(bar1, next1) - bar1)
            sym[0, band] = new0
            sym[1, band] = new1
            sym[2, band] = new2
            grad[0, band] = p0 - 0.25 * bar0
            grad[1, band] = p1 - 0.25 * bar1
            norm = norm + (new0 * new0 + new1 * new1 + 2.0 * (new2 * new2))
        return norm

    def mate_copy(which):
        return remote(norms.at[which, 1 - core], mate_in.at[which], mate_send.at[which], mate_recv.at[which], band=mate)

    def chip_copy(which, peer, slot):
        return remote(
            chip_sum.at[which], chip_in.at[which, slot],
            chip_send.at[which, peer // 2], chip_recv.at[which, slot], band=peer,
        )

    def back_copy(which, half):
        return remote(scales.at[which, core], scales.at[which, half], back_send.at[which], back_recv.at[which], band=mate)

    def send_norm(which, norm):
        norms[which, 0] = norm[:8]
        norms[which, 1] = norm[8:]
        mate_copy(which).start()

    def send_chip(which):
        mate_copy(which).wait()
        total = norms[which, core] + mate_in[which]
        chip_sum[which] = total
        chip_in[which, chip] = total
        for peer in peers:
            chip_copy(which, peer, chip).start()

    def send_scale(which, bound):
        for peer in peers:
            chip_copy(which, peer, peer // 2).wait()
        total = chip_in[which, 0]
        for other in range(1, chip_count):
            total = total + chip_in[which, other]
        scales[which, core] = 1.0 / jnp.maximum(1.0, jnp.sqrt(total) * (1.0 / bound))
        back_copy(which, core).start()

    norm_sym = lax.fori_loop(0, bands // 2, symmetric, jnp.zeros((rows, cols), F32))
    send_norm(0, norm_sym)

    def gather_weights(band, carry):
        gather_w[band] = toeplitz_gather(table, index_ref[band])
        return carry

    lax.fori_loop(0, bands, gather_weights, 0)
    pl.when(chip < chip_count - 1)(lambda: pl.semaphore_wait(ready, chip_count - 1 - chip))
    send_chip(0)

    def first_order(c, norm):
        wait_recv(near_copies(c))
        for k in range(CHUNK):
            band = c * CHUNK + k
            part = bar[band]
            from_up, from_dn = near_from_up[c, k], near_from_dn[c, k]
            top = part[:8] + jnp.where(tile_line == 7, 0.0, not_top * from_up)
            end = part[8:] + jnp.where(tile_line == 0, 0.0, not_end * from_dn)
            own = jnp.concatenate([top, end], 0)
            bar[band] = own
            img[band] = 0.5 * (img[band] + own)
            following = not_end * (near_from_dn[c, k, pl.ds(0, 1), :] + near_dn[c, k, pl.ds(0, 1), :])
            new0 = grad[0, band] + 0.25 * (row_after(own, following) - own)
            new1 = grad[1, band] + 0.25 * (column_after(own) - own)
            grad[0, band] = new0
            grad[1, band] = new1
            norm = norm + (new0 * new0 + new1 * new1)
        return norm

    norm_grad = lax.fori_loop(0, chunks, first_order, jnp.zeros((rows, cols), F32))
    send_norm(1, norm_grad)
    pl.when(chip >= chip_count // 2)(lambda: lax.fori_loop(0, 1, start_far, None))
    load_obs.wait()
    send_chip(1)
    pl.when(chip >= chip_count // 2)(lambda: lax.fori_loop(1, chunks, start_far, None))

    def forward(c, carry):
        wait_recv(far_copies(c))
        for k in range(CHUNK):
            band = c * CHUNK + k
            middle = (tile_line >= 1) & (tile_line <= 6)
            near = pl.ds(7 + 6 * k, 8)
            above = jnp.where(middle, far_from_up[c, near, :], near_from_up[c, k])
            above = not_top * jnp.where(tile_line == 0, 0.0, above + near_up[c, k])
            below = jnp.where(middle, far_from_dn[c, near, :], near_from_dn[c, k])
            below = not_end * jnp.where(tile_line == 7, 0.0, below + near_dn[c, k])
            pairs = padded_shifts(jnp.concatenate([bar[band], above, below], 0))
            highs, lows = [pair[0] for pair in pairs], [pair[1] for pair in pairs]
            stacked = jnp.concatenate(highs + lows + highs, 0)
            product = jnp.dot(gather_w[band], stacked, preferred_element_type=F32)
            blurred = gather_shifts(product, rows, cols)
            data[band] = (data[band] + (blurred - STEP_DUAL * obs[band])) * (1.0 / (1.0 + STEP_DUAL / FIDELITY))
        return carry

    lax.fori_loop(0, chunks, forward, 0)
    send_scale(0, BOUND_SECOND)
    send_scale(1, BOUND_FIRST)

    wait_send(line_copies())

    def finish(c, carry):
        wait_send(near_copies(c))
        wait_send(far_copies(c))
        return carry

    lax.fori_loop(0, chunks, finish, 0)
    for which in range(2):
        back_copy(which, 1 - core).wait()


def finish_kernel(
    img, vec, grad, sym, data, scales,
    image_out, vector_out, grad_out, sym_out, data_out,
    scaled_sym, scaled_grad, plain_sem, sym_sem, grad_sem,
):
    plain = [
        pltpu.make_async_copy(source, target, plain_sem.at[k])
        for k, (source, target) in enumerate(((vec, vector_out), (img, image_out), (data, data_out)))
    ]
    for copy in plain:
        copy.start()
    chunks = img.shape[0] // CHUNK
    factor_sym = jnp.concatenate([scales[0, 0], scales[0, 1]], 0)
    factor_grad = jnp.concatenate([scales[1, 0], scales[1, 1]], 0)

    def stores(c):
        part = pl.ds(c * CHUNK, CHUNK)
        return (
            pltpu.make_async_copy(scaled_sym.at[:, part], sym_out.at[:, part], sym_sem.at[c]),
            pltpu.make_async_copy(scaled_grad.at[:, part], grad_out.at[:, part], grad_sem.at[c]),
        )

    def scale(c, carry):
        for k in range(CHUNK):
            band = c * CHUNK + k
            for part in range(3):
                scaled_sym[part, band] = sym[part, band] * factor_sym
            for part in range(2):
                scaled_grad[part, band] = grad[part, band] * factor_grad
        for copy in stores(c):
            copy.start()
        return carry

    lax.fori_loop(0, chunks, scale, 0)

    def wait(c, carry):
        for copy in stores(c):
            copy.wait()
        return carry

    lax.fori_loop(0, chunks, wait, 0)
    for copy in plain:
        copy.wait()


def body(band_axis, row_axis, observed, image, vector_field, dual_grad, dual_sym, dual_data, kernels, kernel_index):
    bands, rows, cols = image.shape
    chunks = bands // CHUNK
    turned = jnp.transpose(kernels, (1, 0, 2))
    size, count, _ = turned.shape
    vmem, hbm, dma = pltpu.VMEM, pltpu.HBM, pltpu.SemaphoreType.DMA
    near, far = (chunks, CHUNK, 8, cols), (chunks, 16 + 6 * CHUNK, cols)
    line, half = (2, bands, cols), (8, cols)
    anywhere = pl.BlockSpec(memory_space=pl.ANY)
    inside = pl.BlockSpec(memory_space=pltpu.VMEM)
    results = (image, vector_field, dual_grad, dual_sym, dual_data)
    inputs = (kernel_index, turned, observed, image, vector_field, dual_grad, dual_sym, dual_data)
    held = pl.pallas_call(
        functools.partial(kernel, bands, rows, cols, band_axis, row_axis),
        out_shape=[vmem(a.shape, F32) for a in results] + [vmem((2, 2, *half), F32)],
        in_specs=[anywhere] * 8,
        out_specs=[inside] * 6,
        scratch_shapes=[
            pltpu.SMEM(kernel_index.shape, jnp.int32),
            vmem((size, count, size), F32),
            vmem((2, 4, count, 128), F32),
            vmem(image.shape, F32),
            vmem(image.shape, F32),
            vmem((bands, 4 * rows, 384), BF16),
        ]
        + [vmem(line, F32)] * 4
        + [vmem(near, F32)] * 4
        + [vmem(far, F32)] * 4
        + [vmem((2, 2, *half), F32), vmem((2, *half), F32), vmem((2, *half), F32), vmem((2, band_axis // 2, *half), F32)]
        + [dma((8,)), dma((1,)), dma((2,)), dma((2,))]
        + [dma((2, chunks))] * 4
        + [dma((2,))] * 2
        + [dma((2, band_axis // 2))] * 2
        + [dma((2,))] * 2
        + [pltpu.SemaphoreType.REGULAR],
        compiler_params=pltpu.CompilerParams(
            collective_id=0, has_side_effects=True, vmem_limit_bytes=24 * 1024 * 1024
        ),
    )(*[pltpu.with_memory_space_constraint(a, hbm) for a in inputs])
    return pl.pallas_call(
        finish_kernel,
        out_shape=[hbm(a.shape, F32) for a in results],
        in_specs=[inside] * 6,
        out_specs=[anywhere] * 5,
        scratch_shapes=[vmem(dual_sym.shape, F32), vmem(dual_grad.shape, F32), dma((3,)), dma((chunks,)), dma((chunks,))],
        compiler_params=pltpu.CompilerParams(vmem_limit_bytes=16 * 1024 * 1024),
    )(*[pltpu.with_memory_space_constraint(a, vmem) for a in held])


def solution(mesh):
    placed = (
        P("band", "row", None),
        P("band", "row", None),
        P(None, "band", "row", None),
        P(None, "band", "row", None),
        P(None, "band", "row", None),
        P("band", "row", None),
        P(),
        P("band"),
    )
    return jax.shard_map(
        functools.partial(body, mesh.shape["band"], mesh.shape["row"]),
        mesh=mesh,
        in_specs=placed,
        out_specs=(
            P("band", "row", None),
            P(None, "band", "row", None),
            P(None, "band", "row", None),
            P(None, "band", "row", None),
            P("band", "row", None),
        ),
        check_vma=False,
    )
```

```python
import functools

import jax
import jax.numpy as jnp
from jax import lax
from jax.experimental import pallas as pl
from jax.experimental.pallas import tpu as pltpu
from jax.sharding import PartitionSpec as P

FIDELITY = 2.0
STEP_DUAL = 0.25
BOUND_FIRST = 16.0
BOUND_SECOND = 24.0
MESH = pl.DeviceIdType.MESH
F32 = jnp.float32
BF16 = jnp.bfloat16
CHUNK = 4


def split(value):
    high = value.astype(BF16)
    return high, (value - high.astype(F32)).astype(BF16)


def build_tables(kernels_ref, table_ref):
    size, count, _ = kernels_ref.shape
    groups = []
    for half in range(2):
        total = jnp.zeros((count, 128), F32)
        for i in range(8 * half, min(size, 8 * half + 8)):
            slab = jnp.concatenate([kernels_ref[i], jnp.zeros((count, 128 - size), F32)], 1)
            total = total + (pltpu.roll(slab, 16 * (i % 8), 1) if i % 8 else slab)
        groups.append(total)
    high, low = split(jnp.concatenate(groups, 1))
    values = jnp.concatenate([high, low], 0)
    line = lax.broadcasted_iota(jnp.int32, (256, 128), 0)
    lane = lax.broadcasted_iota(jnp.int32, (256, 128), 1)
    b, i = lane // 32, lane % 32
    for t, factor in enumerate((-0.5, STEP_DUAL)):
        for a in range(4):
            j = 4 * a + b
            place = 16 * (size - 1 - i) + size - 1 - j if t == 0 else 16 * i + j
            place = jnp.where((i < size) & (j < size), place, -1)
            chosen = jnp.where(line == place, 1.0, 0.0).astype(BF16)
            both = jnp.dot(values, chosen, preferred_element_type=F32)
            table_ref[t, a] = factor * (both[:count] + both[count:])


def table_row(table_ref, t, a, index):
    return jnp.broadcast_to(table_ref[t, a, pl.ds(index, 1), :], (8, 128))


def toeplitz_scatter(table_ref, index):
    lane = lax.broadcasted_iota(jnp.int32, (8, 128), 1)
    first = lane % 32 < 16
    groups = []
    for a in range(4):
        row = table_row(table_ref, 0, a, index)
        for base in (0, 8, -8, 16):
            moved = pltpu.roll(row, (base - 7) % 128, 1, stride=1, stride_axis=0)
            groups.append(jnp.where(first, moved, pltpu.roll(moved, 16, 1)))
    return jnp.concatenate(split(jnp.concatenate(groups, 0)), 1)


def toeplitz_gather(table_ref, index):
    lane = lax.broadcasted_iota(jnp.int32, (8, 128), 1) % 32
    groups = []
    for a in range(4):
        row = table_row(table_ref, 1, a, index)
        for base in (0, 8):
            own = pltpu.roll(row, (base - 7) % 128, 1, stride=1, stride_axis=0)
            above = pltpu.roll(row, base + 17, 1, stride=1, stride_axis=0)
            below = pltpu.roll(row, base + 1, 1, stride=1, stride_axis=0)
            groups.append(jnp.where(lane < 16, own, jnp.where(lane < 24, above, below)))
    high, low = split(jnp.concatenate(groups, 0))
    return jnp.concatenate([high, high, low], 1)


def padded_shifts(field):
    rows, cols = field.shape
    wide = jnp.concatenate([field, jnp.zeros((rows, 128), F32)], 1)
    return [split(wide if b == 3 else pltpu.roll(wide, 3 - b, 1)) for b in range(4)]


def gather_shifts(product, rows, cols):
    width = product.shape[1]
    total = product[rows : 2 * rows]
    for a in (0, 2, 3):
        total = total + pltpu.roll(product[a * rows : (a + 1) * rows], (4 - 4 * a) % width, 1)
    return total[:, :cols]


def column_before(field):
    lane = lax.broadcasted_iota(jnp.int32, field.shape, 1)
    return jnp.where(lane == 0, 0.0, pltpu.roll(field, 1, 1))


def column_after(field):
    cols = field.shape[1]
    lane = lax.broadcasted_iota(jnp.int32, field.shape, 1)
    return jnp.where(lane == cols - 1, 0.0, pltpu.roll(field, cols - 1, 1))


def row_before(field, first):
    line = lax.broadcasted_iota(jnp.int32, field.shape, 0)
    return jnp.where(line == 0, first, pltpu.roll(field, 1, 0))


def row_after(field, last):
    rows = field.shape[0]
    line = lax.broadcasted_iota(jnp.int32, field.shape, 0)
    return jnp.where(line == rows - 1, last, pltpu.roll(field, rows - 1, 0))


def kernel(
    bands, rows, cols, band_axis, row_axis,
    index_hbm, kernels_hbm, observed_hbm, image_hbm, vector_hbm, grad_hbm, sym_hbm, data_hbm,
    img, vec, grad, sym, data, scales,
    index_ref, kernels_ref, table, obs, bar, gather_w,
    line_up, line_dn, line_from_dn, line_from_up,
    near_up, near_dn, near_from_dn, near_from_up,
    far_up, far_dn, far_from_dn, far_from_up,
    norms, mate_in, chip_sum, chip_in,
    in_sem, data_sem, line_send, line_recv, near_send, near_recv, far_send, far_recv,
    mate_send, mate_recv, chip_send, chip_recv, back_send, back_recv, ready,
):
    me_row, me_band = lax.axis_index("row"), lax.axis_index("band")
    core, chip = lax.rem(me_band, 2), me_band // 2
    mate = me_band + 1 - 2 * core
    chip_count = band_axis // 2
    peers = [lax.rem(me_band + 2 * k, band_axis) for k in range(1, chip_count)]
    has_up, has_down = me_row > 0, me_row < row_axis - 1
    up, down = me_row - 1, me_row + 1
    not_top = jnp.where(has_up, 1.0, 0.0).astype(F32)
    not_end = jnp.where(has_down, 1.0, 0.0).astype(F32)
    chunks = bands // CHUNK

    barrier = pltpu.get_barrier_semaphore()

    def greet(**target):
        pl.semaphore_signal(barrier, inc=1, device_id=target, device_id_type=MESH)

    pl.when(has_up)(lambda: greet(row=up))
    pl.when(has_down)(lambda: greet(row=down))
    greet(band=mate)
    for peer in peers:
        pl.when(peer > me_band)(functools.partial(greet, band=peer))

    def fetch(source, target, sem):
        copy = pltpu.make_async_copy(source, target, sem)
        copy.start()
        return copy

    load_index = fetch(index_hbm, index_ref, in_sem.at[0])
    load_kernels = fetch(kernels_hbm, kernels_ref, in_sem.at[1])
    def fetch_rows(source, target, first, sem):
        part = (slice(None), slice(None), pl.ds(first, 8))
        return fetch(source.at[part], target.at[part], sem)

    fields = ((sym_hbm, sym), (grad_hbm, grad), (vector_hbm, vec))
    load_upper = [fetch_rows(*pair, 0, in_sem.at[2 + k]) for k, pair in enumerate(fields)]
    load_lower = [fetch_rows(*pair, 8, in_sem.at[5 + k]) for k, pair in enumerate(fields)]
    load_data = fetch(data_hbm, data, in_sem.at[8])
    load_img = fetch(image_hbm, img, in_sem.at[9])
    load_obs = fetch(observed_hbm, obs, in_sem.at[10])

    def remote(source, target, send, recv, **which):
        return pltpu.make_async_remote_copy(
            src_ref=source, dst_ref=target, send_sem=send, recv_sem=recv,
            device_id=which, device_id_type=MESH,
        )

    def line_copies():
        return (
            remote(line_up, line_from_dn, line_send.at[0], line_recv.at[0], row=up),
            remote(line_dn, line_from_up, line_send.at[1], line_recv.at[1], row=down),
        )

    def near_copies(c):
        return (
            remote(near_up.at[c], near_from_dn.at[c], near_send.at[0, c], near_recv.at[0, c], row=up),
            remote(near_dn.at[c], near_from_up.at[c], near_send.at[1, c], near_recv.at[1, c], row=down),
        )

    def far_copies(c):
        body = pl.ds(8, 6 * CHUNK)
        return (
            remote(far_up.at[c, body], far_from_dn.at[c, body], far_send.at[0, c], far_recv.at[0, c], row=up),
            remote(far_dn.at[c, body], far_from_up.at[c, body], far_send.at[1, c], far_recv.at[1, c], row=down),
        )

    def start(copies):
        pl.when(has_up)(copies[0].start)
        pl.when(has_down)(copies[1].start)

    def wait_recv(copies):
        pl.when(has_down)(copies[0].wait_recv)
        pl.when(has_up)(copies[1].wait_recv)

    def wait_send(copies):
        pl.when(has_up)(copies[0].wait_send)
        pl.when(has_down)(copies[1].wait_send)

    @pl.when(jnp.logical_not(has_up))
    def _():
        for ref in (line_from_up, near_from_up, far_from_up):
            ref[...] = jnp.zeros(ref.shape, F32)

    @pl.when(jnp.logical_not(has_down))
    def _():
        for ref in (line_from_dn, near_from_dn, far_from_dn):
            ref[...] = jnp.zeros(ref.shape, F32)

    load_kernels.wait()
    build_tables(kernels_ref, table)

    for load in load_upper:
        load.wait()

    def lines_of(ref, part, row):
        return ref[part, :, row, :]

    q0, q1, cross = [lines_of(sym, part, 0) for part in range(3)]
    line_up[0] = lines_of(vec, 0, 0) + 0.5 * (q0 - (column_before(cross) - cross) + lines_of(grad, 0, 0))
    line_up[1] = lines_of(vec, 1, 0) + 0.5 * (cross - (column_before(q1) - q1) + lines_of(grad, 1, 0))
    pl.semaphore_wait(barrier, 1 + chip + has_up.astype(jnp.int32) + has_down.astype(jnp.int32))

    def answer(peer):
        pl.semaphore_signal(ready, inc=1, device_id={"band": peer}, device_id_type=MESH)

    for peer in peers:
        pl.when(peer < me_band)(functools.partial(answer, peer))
    pl.when(has_up)(line_copies()[0].start)
    for load in load_lower:
        load.wait()
    line_dn[0] = lines_of(sym, 0, rows - 1)
    line_dn[1] = lines_of(sym, 2, rows - 1)
    pl.when(has_down)(line_copies()[1].start)

    load_index.wait()
    load_data.wait()
    load_img.wait()
    tile_line = lax.broadcasted_iota(jnp.int32, (8, cols), 0)

    def adjoint(c, carry):
        for k in range(CHUNK):
            band = c * CHUNK + k
            parts = [part for pair in padded_shifts(data[band]) for part in pair]
            stacked = jnp.concatenate(parts + parts, 0)
            weights = toeplitz_scatter(table, index_ref[band])
            product = jnp.dot(weights, stacked, preferred_element_type=F32)
            total = gather_shifts(product, 2 * rows, cols)
            p0, p1 = grad[0, band], grad[1, band]
            own = img[band] + total[:rows] - 0.5 * (row_before(p0, 0.0) - p0 + column_before(p1) - p1)
            bar[band] = own
            above, below = total[rows : rows + 8], total[rows + 8 : rows + 16]
            near_up[c, k] = jnp.where(tile_line == 0, own[:8], above)
            below = below - jnp.where(tile_line == 0, 0.5 * pltpu.roll(p0[8:], 1, 0), 0.0)
            near_dn[c, k] = jnp.where(tile_line == 7, own[8:], below)
            far_up[c, pl.ds(8 + 6 * k, 6), :] = own[1:7]
            far_dn[c, pl.ds(8 + 6 * k, 6), :] = own[9:15]
        start(near_copies(c))
        return carry

    lax.fori_loop(0, chunks, adjoint, 0)

    def start_far(c, carry):
        start(far_copies(c))


    pl.when(chip < chip_count // 2)(lambda: lax.fori_loop(0, chunks, start_far, None))

    wait_recv(line_copies())

    def symmetric(step, norm):
        for k in range(2):
            band = 2 * step + k
            q0, q1, q2 = sym[0, band], sym[1, band], sym[2, band]
            p0, p1 = grad[0, band], grad[1, band]
            v0, v1 = vec[0, band], vec[1, band]
            here = pl.ds(band, 1)
            prev0, prev2 = not_top * line_from_up[0, here, :], not_top * line_from_up[1, here, :]
            step0 = 0.25 * (row_before(q0, prev0) - q0 + column_before(q2) - q2 - p0)
            step1 = 0.25 * (column_before(q1) - q1 + row_before(q2, prev2) - q2 - p1)
            vec[0, band] = v0 - step0
            vec[1, band] = v1 - step1
            bar0, bar1 = v0 - 2.0 * step0, v1 - 2.0 * step1
            end = pl.ds(rows - 1, 1)
            next0 = not_end * (line_from_dn[0, here, :] - 0.5 * sym[0, band, end, :])
            next1 = not_end * (line_from_dn[1, here, :] - 0.5 * sym[2, band, end, :])
            new0 = q0 + 0.25 * (row_after(bar0, next0) - bar0)
            new1 = q1 + 0.25 * (column_after(bar1) - bar1)
            new2 = q2 + 0.125 * (column_after(bar0) - bar0 + row_after(bar1, next1) - bar1)
            sym[0, band] = new0
            sym[1, band] = new1
            sym[2, band] = new2
            grad[0, band] = p0 - 0.25 * bar0
            grad[1, band] = p1 - 0.25 * bar1
            norm = norm + (new0 * new0 + new1 * new1 + 2.0 * (new2 * new2))
        return norm

    def mate_copy(which):
        return remote(norms.at[which, 1 - core], mate_in.at[which], mate_send.at[which], mate_recv.at[which], band=mate)

    def chip_copy(which, peer, slot):
        return remote(
            chip_sum.at[which], chip_in.at[which, slot],
            chip_send.at[which, peer // 2], chip_recv.at[which, slot], band=peer,
        )

    def back_copy(which, half):
        return remote(scales.at[which, core], scales.at[which, half], back_send.at[which], back_recv.at[which], band=mate)

    def send_norm(which, norm):
        norms[which, 0] = norm[:8]
        norms[which, 1] = norm[8:]
        mate_copy(which).start()

    def send_chip(which):
        mate_copy(which).wait()
        total = norms[which, core] + mate_in[which]
        chip_sum[which] = total
        chip_in[which, chip] = total
        for peer in peers:
            chip_copy(which, peer, chip).start()

    def send_scale(which, bound):
        for peer in peers:
            chip_copy(which, peer, peer // 2).wait()
        total = chip_in[which, 0]
        for other in range(1, chip_count):
            total = total + chip_in[which, other]
        scales[which, core] = 1.0 / jnp.maximum(1.0, jnp.sqrt(total) * (1.0 / bound))
        back_copy(which, core).start()

    norm_sym = lax.fori_loop(0, bands // 2, symmetric, jnp.zeros((rows, cols), F32))
    send_norm(0, norm_sym)

    def gather_weights(band, carry):
        gather_w[band] = toeplitz_gather(table, index_ref[band])
        return carry

    lax.fori_loop(0, bands, gather_weights, 0)
    pl.when(chip < chip_count - 1)(lambda: pl.semaphore_wait(ready, chip_count - 1 - chip))
    send_chip(0)

    def first_order(c, norm):
        wait_recv(near_copies(c))
        for k in range(CHUNK):
            band = c * CHUNK + k
            part = bar[band]
            from_up, from_dn = near_from_up[c, k], near_from_dn[c, k]
            top = part[:8] + jnp.where(tile_line == 7, 0.0, not_top * from_up)
            end = part[8:] + jnp.where(tile_line == 0, 0.0, not_end * from_dn)
            own = jnp.concatenate([top, end], 0)
            bar[band] = own
            img[band] = 0.5 * (img[band] + own)
            following = not_end * (near_from_dn[c, k, pl.ds(0, 1), :] + near_dn[c, k, pl.ds(0, 1), :])
            new0 = grad[0, band] + 0.25 * (row_after(own, following) - own)
            new1 = grad[1, band] + 0.25 * (column_after(own) - own)
            grad[0, band] = new0
            grad[1, band] = new1
            norm = norm + (new0 * new0 + new1 * new1)
        return norm

    norm_grad = lax.fori_loop(0, chunks, first_order, jnp.zeros((rows, cols), F32))
    send_norm(1, norm_grad)
    pl.when(chip >= chip_count // 2)(lambda: lax.fori_loop(0, 1, start_far, None))
    load_obs.wait()
    send_chip(1)
    pl.when(chip >= chip_count // 2)(lambda: lax.fori_loop(1, chunks, start_far, None))

    def forward(c, carry):
        wait_recv(far_copies(c))
        for k in range(CHUNK):
            band = c * CHUNK + k
            middle = (tile_line >= 1) & (tile_line <= 6)
            near = pl.ds(7 + 6 * k, 8)
            above = jnp.where(middle, far_from_up[c, near, :], near_from_up[c, k])
            above = not_top * jnp.where(tile_line == 0, 0.0, above + near_up[c, k])
            below = jnp.where(middle, far_from_dn[c, near, :], near_from_dn[c, k])
            below = not_end * jnp.where(tile_line == 7, 0.0, below + near_dn[c, k])
            pairs = padded_shifts(jnp.concatenate([bar[band], above, below], 0))
            highs, lows = [pair[0] for pair in pairs], [pair[1] for pair in pairs]
            stacked = jnp.concatenate(highs + lows + highs, 0)
            product = jnp.dot(gather_w[band], stacked, preferred_element_type=F32)
            blurred = gather_shifts(product, rows, cols)
            data[band] = (data[band] + (blurred - STEP_DUAL * obs[band])) * (1.0 / (1.0 + STEP_DUAL / FIDELITY))
        return carry

    lax.fori_loop(0, chunks, forward, 0)
    send_scale(0, BOUND_SECOND)
    send_scale(1, BOUND_FIRST)

    wait_send(line_copies())

    def finish(c, carry):
        wait_send(near_copies(c))
        wait_send(far_copies(c))
        return carry

    lax.fori_loop(0, chunks, finish, 0)
    for which in range(2):
        back_copy(which, 1 - core).wait()


def finish_kernel(
    img, vec, grad, sym, data, scales,
    image_out, vector_out, grad_out, sym_out, data_out,
    scaled_sym, scaled_grad, plain_sem, sym_sem, grad_sem,
):
    plain = [
        pltpu.make_async_copy(source, target, plain_sem.at[k])
        for k, (source, target) in enumerate(((vec, vector_out), (img, image_out), (data, data_out)))
    ]
    for copy in plain:
        copy.start()
    chunks = img.shape[0] // CHUNK
    factor_sym = jnp.concatenate([scales[0, 0], scales[0, 1]], 0)
    factor_grad = jnp.concatenate([scales[1, 0], scales[1, 1]], 0)

    def stores(c):
        part = pl.ds(c * CHUNK, CHUNK)
        return (
            pltpu.make_async_copy(scaled_sym.at[:, part], sym_out.at[:, part], sym_sem.at[c]),
            pltpu.make_async_copy(scaled_grad.at[:, part], grad_out.at[:, part], grad_sem.at[c]),
        )

    def scale(c, carry):
        for k in range(CHUNK):
            band = c * CHUNK + k
            for part in range(3):
                scaled_sym[part, band] = sym[part, band] * factor_sym
            for part in range(2):
                scaled_grad[part, band] = grad[part, band] * factor_grad
        for copy in stores(c):
            copy.start()
        return carry

    lax.fori_loop(0, chunks, scale, 0)

    def wait(c, carry):
        for copy in stores(c):
            copy.wait()
        return carry

    lax.fori_loop(0, chunks, wait, 0)
    for copy in plain:
        copy.wait()


def body(band_axis, row_axis, observed, image, vector_field, dual_grad, dual_sym, dual_data, kernels, kernel_index):
    bands, rows, cols = image.shape
    chunks = bands // CHUNK
    turned = jnp.transpose(kernels, (1, 0, 2))
    size, count, _ = turned.shape
    vmem, hbm, dma = pltpu.VMEM, pltpu.HBM, pltpu.SemaphoreType.DMA
    near, far = (chunks, CHUNK, 8, cols), (chunks, 16 + 6 * CHUNK, cols)
    line, half = (2, bands, cols), (8, cols)
    anywhere = pl.BlockSpec(memory_space=pl.ANY)
    inside = pl.BlockSpec(memory_space=pltpu.VMEM)
    results = (image, vector_field, dual_grad, dual_sym, dual_data)
    inputs = (kernel_index, turned, observed, image, vector_field, dual_grad, dual_sym, dual_data)
    held = pl.pallas_call(
        functools.partial(kernel, bands, rows, cols, band_axis, row_axis),
        out_shape=[vmem(a.shape, F32) for a in results] + [vmem((2, 2, *half), F32)],
        in_specs=[anywhere] * 8,
        out_specs=[inside] * 6,
        scratch_shapes=[
            pltpu.SMEM(kernel_index.shape, jnp.int32),
            vmem((size, count, size), F32),
            vmem((2, 4, count, 128), F32),
            vmem(image.shape, F32),
            vmem(image.shape, F32),
            vmem((bands, 4 * rows, 384), BF16),
        ]
        + [vmem(line, F32)] * 4
        + [vmem(near, F32)] * 4
        + [vmem(far, F32)] * 4
        + [vmem((2, 2, *half), F32), vmem((2, *half), F32), vmem((2, *half), F32), vmem((2, band_axis // 2, *half), F32)]
        + [dma((11,)), dma((1,)), dma((2,)), dma((2,))]
        + [dma((2, chunks))] * 4
        + [dma((2,))] * 2
        + [dma((2, band_axis // 2))] * 2
        + [dma((2,))] * 2
        + [pltpu.SemaphoreType.REGULAR],
        compiler_params=pltpu.CompilerParams(
            collective_id=0, has_side_effects=True, vmem_limit_bytes=24 * 1024 * 1024
        ),
    )(*[pltpu.with_memory_space_constraint(a, hbm) for a in inputs])
    return pl.pallas_call(
        finish_kernel,
        out_shape=[hbm(a.shape, F32) for a in results],
        in_specs=[inside] * 6,
        out_specs=[anywhere] * 5,
        scratch_shapes=[vmem(dual_sym.shape, F32), vmem(dual_grad.shape, F32), dma((3,)), dma((chunks,)), dma((chunks,))],
        compiler_params=pltpu.CompilerParams(vmem_limit_bytes=16 * 1024 * 1024),
    )(*[pltpu.with_memory_space_constraint(a, vmem) for a in held])


def solution(mesh):
    placed = (
        P("band", "row", None),
        P("band", "row", None),
        P(None, "band", "row", None),
        P(None, "band", "row", None),
        P(None, "band", "row", None),
        P("band", "row", None),
        P(),
        P("band"),
    )
    return jax.shard_map(
        functools.partial(body, mesh.shape["band"], mesh.shape["row"]),
        mesh=mesh,
        in_specs=placed,
        out_specs=(
            P("band", "row", None),
            P(None, "band", "row", None),
            P(None, "band", "row", None),
            P(None, "band", "row", None),
            P("band", "row", None),
        ),
        check_vma=False,
    )
```

```python
import functools

import jax
import jax.numpy as jnp
from jax import lax
from jax.experimental import pallas as pl
from jax.experimental.pallas import tpu as pltpu
from jax.sharding import PartitionSpec as P

FIDELITY = 2.0
STEP_DUAL = 0.25
BOUND_FIRST = 16.0
BOUND_SECOND = 24.0
MESH = pl.DeviceIdType.MESH
F32 = jnp.float32
BF16 = jnp.bfloat16
CHUNK = 4


def split(value):
    high = value.astype(BF16)
    return high, (value - high.astype(F32)).astype(BF16)


def build_tables(kernels_ref, table_ref):
    size, count, _ = kernels_ref.shape
    groups = []
    for half in range(2):
        total = jnp.zeros((count, 128), F32)
        for i in range(8 * half, min(size, 8 * half + 8)):
            slab = jnp.concatenate([kernels_ref[i], jnp.zeros((count, 128 - size), F32)], 1)
            total = total + (pltpu.roll(slab, 16 * (i % 8), 1) if i % 8 else slab)
        groups.append(total)
    high, low = split(jnp.concatenate(groups, 1))
    values = jnp.concatenate([high, low], 0)
    line = lax.broadcasted_iota(jnp.int32, (256, 128), 0)
    lane = lax.broadcasted_iota(jnp.int32, (256, 128), 1)
    b, i = lane // 32, lane % 32
    for t, factor in enumerate((-0.5, STEP_DUAL)):
        for a in range(4):
            j = 4 * a + b
            place = 16 * (size - 1 - i) + size - 1 - j if t == 0 else 16 * i + j
            place = jnp.where((i < size) & (j < size), place, -1)
            chosen = jnp.where(line == place, 1.0, 0.0).astype(BF16)
            both = jnp.dot(values, chosen, preferred_element_type=F32)
            table_ref[t, a] = factor * (both[:count] + both[count:])


def table_row(table_ref, t, a, index):
    return jnp.broadcast_to(table_ref[t, a, pl.ds(index, 1), :], (8, 128))


def toeplitz_scatter(table_ref, index):
    lane = lax.broadcasted_iota(jnp.int32, (8, 128), 1)
    first = lane % 32 < 16
    groups = []
    for a in range(4):
        row = table_row(table_ref, 0, a, index)
        for base in (0, 8, -8, 16):
            moved = pltpu.roll(row, (base - 7) % 128, 1, stride=1, stride_axis=0)
            groups.append(jnp.where(first, moved, pltpu.roll(moved, 16, 1)))
    return jnp.concatenate(split(jnp.concatenate(groups, 0)), 1)


def toeplitz_gather(table_ref, index):
    lane = lax.broadcasted_iota(jnp.int32, (8, 128), 1) % 32
    groups = []
    for a in range(4):
        row = table_row(table_ref, 1, a, index)
        for base in (0, 8):
            own = pltpu.roll(row, (base - 7) % 128, 1, stride=1, stride_axis=0)
            above = pltpu.roll(row, base + 17, 1, stride=1, stride_axis=0)
            below = pltpu.roll(row, base + 1, 1, stride=1, stride_axis=0)
            groups.append(jnp.where(lane < 16, own, jnp.where(lane < 24, above, below)))
    high, low = split(jnp.concatenate(groups, 0))
    return jnp.concatenate([high, high, low], 1)


def padded_shifts(field):
    rows, cols = field.shape
    wide = jnp.concatenate([field, jnp.zeros((rows, 128), F32)], 1)
    return [split(wide if b == 3 else pltpu.roll(wide, 3 - b, 1)) for b in range(4)]


def gather_shifts(product, rows, cols):
    width = product.shape[1]
    total = product[rows : 2 * rows]
    for a in (0, 2, 3):
        total = total + pltpu.roll(product[a * rows : (a + 1) * rows], (4 - 4 * a) % width, 1)
    return total[:, :cols]


def column_before(field):
    lane = lax.broadcasted_iota(jnp.int32, field.shape, 1)
    return jnp.where(lane == 0, 0.0, pltpu.roll(field, 1, 1))


def column_after(field):
    cols = field.shape[1]
    lane = lax.broadcasted_iota(jnp.int32, field.shape, 1)
    return jnp.where(lane == cols - 1, 0.0, pltpu.roll(field, cols - 1, 1))


def row_before(field, first):
    line = lax.broadcasted_iota(jnp.int32, field.shape, 0)
    return jnp.where(line == 0, first, pltpu.roll(field, 1, 0))


def row_after(field, last):
    rows = field.shape[0]
    line = lax.broadcasted_iota(jnp.int32, field.shape, 0)
    return jnp.where(line == rows - 1, last, pltpu.roll(field, rows - 1, 0))


def kernel(
    bands, rows, cols, band_axis, row_axis,
    index_hbm, kernels_hbm, observed_hbm, image_hbm, vector_hbm, grad_hbm, sym_hbm, data_hbm,
    img, vec, grad, sym, data, scales,
    index_ref, kernels_ref, table, obs, bar, gather_w,
    line_up, line_dn, line_from_dn, line_from_up,
    near_up, near_dn, near_from_dn, near_from_up,
    far_up, far_dn, far_from_dn, far_from_up,
    norms, mate_in, chip_sum, chip_in,
    in_sem, data_sem, line_send, line_recv, near_send, near_recv, far_send, far_recv,
    mate_send, mate_recv, chip_send, chip_recv, cross_send, back_send, back_recv, ready,
):
    me_row, me_band = lax.axis_index("row"), lax.axis_index("band")
    core, chip = lax.rem(me_band, 2), me_band // 2
    mate = me_band + 1 - 2 * core
    chip_count = band_axis // 2
    peers = [lax.rem(me_band + 2 * k, band_axis) for k in range(1, chip_count)]
    has_up, has_down = me_row > 0, me_row < row_axis - 1
    up, down = me_row - 1, me_row + 1
    not_top = jnp.where(has_up, 1.0, 0.0).astype(F32)
    not_end = jnp.where(has_down, 1.0, 0.0).astype(F32)
    chunks = bands // CHUNK

    barrier = pltpu.get_barrier_semaphore()

    def greet(**target):
        pl.semaphore_signal(barrier, inc=1, device_id=target, device_id_type=MESH)

    pl.when(has_up)(lambda: greet(row=up))
    pl.when(has_down)(lambda: greet(row=down))
    greet(band=mate)
    for peer in peers:
        pl.when(peer > me_band)(functools.partial(greet, band=peer))

    @pl.when(chip == 0)
    def _():
        for other in range(1, chip_count):
            greet(band=2 * other + 1 - core)


    def fetch(source, target, sem):
        copy = pltpu.make_async_copy(source, target, sem)
        copy.start()
        return copy

    load_index = fetch(index_hbm, index_ref, in_sem.at[0])
    load_kernels = fetch(kernels_hbm, kernels_ref, in_sem.at[1])
    def fetch_rows(source, target, first, sem):
        part = (slice(None), slice(None), pl.ds(first, 8))
        return fetch(source.at[part], target.at[part], sem)

    fields = ((sym_hbm, sym), (grad_hbm, grad), (vector_hbm, vec))
    load_upper = [fetch_rows(*pair, 0, in_sem.at[2 + k]) for k, pair in enumerate(fields)]
    load_lower = [fetch_rows(*pair, 8, in_sem.at[5 + k]) for k, pair in enumerate(fields)]
    load_data = fetch(data_hbm, data, in_sem.at[8])
    load_img = fetch(image_hbm, img, in_sem.at[9])
    load_obs = fetch(observed_hbm, obs, in_sem.at[10])

    def remote(source, target, send, recv, **which):
        return pltpu.make_async_remote_copy(
            src_ref=source, dst_ref=target, send_sem=send, recv_sem=recv,
            device_id=which, device_id_type=MESH,
        )

    def line_copies():
        return (
            remote(line_up, line_from_dn, line_send.at[0], line_recv.at[0], row=up),
            remote(line_dn, line_from_up, line_send.at[1], line_recv.at[1], row=down),
        )

    def near_copies(c):
        return (
            remote(near_up.at[c], near_from_dn.at[c], near_send.at[0, c], near_recv.at[0, c], row=up),
            remote(near_dn.at[c], near_from_up.at[c], near_send.at[1, c], near_recv.at[1, c], row=down),
        )

    def far_copies(c):
        body = pl.ds(8, 6 * CHUNK)
        return (
            remote(far_up.at[c, body], far_from_dn.at[c, body], far_send.at[0, c], far_recv.at[0, c], row=up),
            remote(far_dn.at[c, body], far_from_up.at[c, body], far_send.at[1, c], far_recv.at[1, c], row=down),
        )

    def start(copies):
        pl.when(has_up)(copies[0].start)
        pl.when(has_down)(copies[1].start)

    def wait_recv(copies):
        pl.when(has_down)(copies[0].wait_recv)
        pl.when(has_up)(copies[1].wait_recv)

    def wait_send(copies):
        pl.when(has_up)(copies[0].wait_send)
        pl.when(has_down)(copies[1].wait_send)

    @pl.when(jnp.logical_not(has_up))
    def _():
        for ref in (line_from_up, near_from_up, far_from_up):
            ref[...] = jnp.zeros(ref.shape, F32)

    @pl.when(jnp.logical_not(has_down))
    def _():
        for ref in (line_from_dn, near_from_dn, far_from_dn):
            ref[...] = jnp.zeros(ref.shape, F32)

    load_kernels.wait()
    build_tables(kernels_ref, table)

    for load in load_upper:
        load.wait()

    def lines_of(ref, part, row):
        return ref[part, :, row, :]

    q0, q1, cross = [lines_of(sym, part, 0) for part in range(3)]
    line_up[0] = lines_of(vec, 0, 0) + 0.5 * (q0 - (column_before(cross) - cross) + lines_of(grad, 0, 0))
    line_up[1] = lines_of(vec, 1, 0) + 0.5 * (cross - (column_before(q1) - q1) + lines_of(grad, 1, 0))
    pl.semaphore_wait(barrier, 1 + chip + (chip > 0).astype(jnp.int32) + has_up.astype(jnp.int32) + has_down.astype(jnp.int32))

    def answer(peer):
        pl.semaphore_signal(ready, inc=1, device_id={"band": peer}, device_id_type=MESH)

    for peer in peers:
        pl.when(peer < me_band)(functools.partial(answer, peer))
    pl.when(has_up)(line_copies()[0].start)
    for load in load_lower:
        load.wait()
    line_dn[0] = lines_of(sym, 0, rows - 1)
    line_dn[1] = lines_of(sym, 2, rows - 1)
    pl.when(has_down)(line_copies()[1].start)

    load_index.wait()
    load_data.wait()
    load_img.wait()
    tile_line = lax.broadcasted_iota(jnp.int32, (8, cols), 0)

    def adjoint(c, carry):
        for k in range(CHUNK):
            band = c * CHUNK + k
            parts = [part for pair in padded_shifts(data[band]) for part in pair]
            stacked = jnp.concatenate(parts + parts, 0)
            weights = toeplitz_scatter(table, index_ref[band])
            product = jnp.dot(weights, stacked, preferred_element_type=F32)
            total = gather_shifts(product, 2 * rows, cols)
            p0, p1 = grad[0, band], grad[1, band]
            own = img[band] + total[:rows] - 0.5 * (row_before(p0, 0.0) - p0 + column_before(p1) - p1)
            bar[band] = own
            above, below = total[rows : rows + 8], total[rows + 8 : rows + 16]
            near_up[c, k] = jnp.where(tile_line == 0, own[:8], above)
            below = below - jnp.where(tile_line == 0, 0.5 * pltpu.roll(p0[8:], 1, 0), 0.0)
            near_dn[c, k] = jnp.where(tile_line == 7, own[8:], below)
            far_up[c, pl.ds(8 + 6 * k, 6), :] = own[1:7]
            far_dn[c, pl.ds(8 + 6 * k, 6), :] = own[9:15]
        start(near_copies(c))
        return carry

    lax.fori_loop(0, chunks, adjoint, 0)

    def start_far(c, carry):
        start(far_copies(c))


    pl.when(chip < chip_count // 2)(lambda: lax.fori_loop(0, chunks, start_far, None))

    wait_recv(line_copies())

    def symmetric(step, norm):
        for k in range(2):
            band = 2 * step + k
            q0, q1, q2 = sym[0, band], sym[1, band], sym[2, band]
            p0, p1 = grad[0, band], grad[1, band]
            v0, v1 = vec[0, band], vec[1, band]
            here = pl.ds(band, 1)
            prev0, prev2 = not_top * line_from_up[0, here, :], not_top * line_from_up[1, here, :]
            step0 = 0.25 * (row_before(q0, prev0) - q0 + column_before(q2) - q2 - p0)
            step1 = 0.25 * (column_before(q1) - q1 + row_before(q2, prev2) - q2 - p1)
            vec[0, band] = v0 - step0
            vec[1, band] = v1 - step1
            bar0, bar1 = v0 - 2.0 * step0, v1 - 2.0 * step1
            end = pl.ds(rows - 1, 1)
            next0 = not_end * (line_from_dn[0, here, :] - 0.5 * sym[0, band, end, :])
            next1 = not_end * (line_from_dn[1, here, :] - 0.5 * sym[2, band, end, :])
            new0 = q0 + 0.25 * (row_after(bar0, next0) - bar0)
            new1 = q1 + 0.25 * (column_after(bar1) - bar1)
            new2 = q2 + 0.125 * (column_after(bar0) - bar0 + row_after(bar1, next1) - bar1)
            sym[0, band] = new0
            sym[1, band] = new1
            sym[2, band] = new2
            grad[0, band] = p0 - 0.25 * bar0
            grad[1, band] = p1 - 0.25 * bar1
            norm = norm + (new0 * new0 + new1 * new1 + 2.0 * (new2 * new2))
        return norm

    def mate_copy(which):
        return remote(norms.at[which, 1 - core], mate_in.at[which], mate_send.at[which], mate_recv.at[which], band=mate)

    def chip_copy(which, peer, slot):
        return remote(
            chip_sum.at[which], chip_in.at[which, core, slot],
            chip_send.at[which, peer // 2], chip_recv.at[which, core, slot], band=peer,
        )

    def cross_copy(which, half, slot):
        return remote(
            chip_sum.at[which], chip_in.at[which, half, slot],
            cross_send.at[which], chip_recv.at[which, half, slot], band=1 - core,
        )

    def back_copy(which, half):
        return remote(scales.at[which, core], scales.at[which, half], back_send.at[which], back_recv.at[which], band=mate)

    def send_norm(which, norm):
        norms[which, 0] = norm[:8]
        norms[which, 1] = norm[8:]
        mate_copy(which).start()

    def send_chip(which):
        mate_copy(which).wait()
        total = norms[which, core] + mate_in[which]
        chip_sum[which] = total
        chip_in[which, core, chip] = total
        cross_copy(which, core, chip).start()
        for peer in peers:
            chip_copy(which, peer, chip).start()

    def scale_half(which, half, bound):
        total = chip_in[which, half, 0]
        for other in range(1, chip_count):
            total = total + chip_in[which, half, other]
        scales[which, half] = 1.0 / jnp.maximum(1.0, jnp.sqrt(total) * (1.0 / bound))

    def send_scale(which, bound):
        for peer in peers:
            chip_copy(which, peer, peer // 2).wait()
        scale_half(which, core, bound)
        pl.when(chip > 0)(back_copy(which, core).start)

    def other_scale(which, bound):
        @pl.when(chip == 0)
        def _():
            for other in range(chip_count):
                cross_copy(which, 1 - core, other).wait_recv()
            scale_half(which, 1 - core, bound)

        pl.when(chip > 0)(back_copy(which, 1 - core).wait)
        cross_copy(which, core, chip).wait_send()

    norm_sym = lax.fori_loop(0, bands // 2, symmetric, jnp.zeros((rows, cols), F32))
    send_norm(0, norm_sym)

    def gather_weights(band, carry):
        gather_w[band] = toeplitz_gather(table, index_ref[band])
        return carry

    lax.fori_loop(0, bands, gather_weights, 0)
    pl.when(chip < chip_count - 1)(lambda: pl.semaphore_wait(ready, chip_count - 1 - chip))
    send_chip(0)

    def first_order(c, norm):
        wait_recv(near_copies(c))
        for k in range(CHUNK):
            band = c * CHUNK + k
            part = bar[band]
            from_up, from_dn = near_from_up[c, k], near_from_dn[c, k]
            top = part[:8] + jnp.where(tile_line == 7, 0.0, not_top * from_up)
            end = part[8:] + jnp.where(tile_line == 0, 0.0, not_end * from_dn)
            own = jnp.concatenate([top, end], 0)
            bar[band] = own
            img[band] = 0.5 * (img[band] + own)
            following = not_end * (near_from_dn[c, k, pl.ds(0, 1), :] + near_dn[c, k, pl.ds(0, 1), :])
            new0 = grad[0, band] + 0.25 * (row_after(own, following) - own)
            new1 = grad[1, band] + 0.25 * (column_after(own) - own)
            grad[0, band] = new0
            grad[1, band] = new1
            norm = norm + (new0 * new0 + new1 * new1)
        return norm

    norm_grad = lax.fori_loop(0, chunks, first_order, jnp.zeros((rows, cols), F32))
    send_norm(1, norm_grad)
    pl.when(chip >= chip_count // 2)(lambda: lax.fori_loop(0, 1, start_far, None))
    load_obs.wait()
    send_chip(1)
    pl.when(chip >= chip_count // 2)(lambda: lax.fori_loop(1, chunks, start_far, None))

    def forward(c, carry):
        wait_recv(far_copies(c))
        for k in range(CHUNK):
            band = c * CHUNK + k
            middle = (tile_line >= 1) & (tile_line <= 6)
            near = pl.ds(7 + 6 * k, 8)
            above = jnp.where(middle, far_from_up[c, near, :], near_from_up[c, k])
            above = not_top * jnp.where(tile_line == 0, 0.0, above + near_up[c, k])
            below = jnp.where(middle, far_from_dn[c, near, :], near_from_dn[c, k])
            below = not_end * jnp.where(tile_line == 7, 0.0, below + near_dn[c, k])
            pairs = padded_shifts(jnp.concatenate([bar[band], above, below], 0))
            highs, lows = [pair[0] for pair in pairs], [pair[1] for pair in pairs]
            stacked = jnp.concatenate(highs + lows + highs, 0)
            product = jnp.dot(gather_w[band], stacked, preferred_element_type=F32)
            blurred = gather_shifts(product, rows, cols)
            data[band] = (data[band] + (blurred - STEP_DUAL * obs[band])) * (1.0 / (1.0 + STEP_DUAL / FIDELITY))
        return carry

    lax.fori_loop(0, chunks, forward, 0)
    send_scale(0, BOUND_SECOND)
    send_scale(1, BOUND_FIRST)

    wait_send(line_copies())

    def finish(c, carry):
        wait_send(near_copies(c))
        wait_send(far_copies(c))
        return carry

    lax.fori_loop(0, chunks, finish, 0)
    other_scale(0, BOUND_SECOND)
    other_scale(1, BOUND_FIRST)


def finish_kernel(
    img, vec, grad, sym, data, scales,
    image_out, vector_out, grad_out, sym_out, data_out,
    scaled_sym, scaled_grad, plain_sem, sym_sem, grad_sem,
):
    plain = [
        pltpu.make_async_copy(source, target, plain_sem.at[k])
        for k, (source, target) in enumerate(((vec, vector_out), (img, image_out), (data, data_out)))
    ]
    for copy in plain:
        copy.start()
    chunks = img.shape[0] // CHUNK
    factor_sym = jnp.concatenate([scales[0, 0], scales[0, 1]], 0)
    factor_grad = jnp.concatenate([scales[1, 0], scales[1, 1]], 0)

    def stores(c):
        part = pl.ds(c * CHUNK, CHUNK)
        return (
            pltpu.make_async_copy(scaled_sym.at[:, part], sym_out.at[:, part], sym_sem.at[c]),
            pltpu.make_async_copy(scaled_grad.at[:, part], grad_out.at[:, part], grad_sem.at[c]),
        )

    def scale(c, carry):
        for k in range(CHUNK):
            band = c * CHUNK + k
            for part in range(3):
                scaled_sym[part, band] = sym[part, band] * factor_sym
            for part in range(2):
                scaled_grad[part, band] = grad[part, band] * factor_grad
        for copy in stores(c):
            copy.start()
        return carry

    lax.fori_loop(0, chunks, scale, 0)

    def wait(c, carry):
        for copy in stores(c):
            copy.wait()
        return carry

    lax.fori_loop(0, chunks, wait, 0)
    for copy in plain:
        copy.wait()


def body(band_axis, row_axis, observed, image, vector_field, dual_grad, dual_sym, dual_data, kernels, kernel_index):
    bands, rows, cols = image.shape
    chunks = bands // CHUNK
    turned = jnp.transpose(kernels, (1, 0, 2))
    size, count, _ = turned.shape
    vmem, hbm, dma = pltpu.VMEM, pltpu.HBM, pltpu.SemaphoreType.DMA
    near, far = (chunks, CHUNK, 8, cols), (chunks, 16 + 6 * CHUNK, cols)
    line, half = (2, bands, cols), (8, cols)
    anywhere = pl.BlockSpec(memory_space=pl.ANY)
    inside = pl.BlockSpec(memory_space=pltpu.VMEM)
    results = (image, vector_field, dual_grad, dual_sym, dual_data)
    inputs = (kernel_index, turned, observed, image, vector_field, dual_grad, dual_sym, dual_data)
    held = pl.pallas_call(
        functools.partial(kernel, bands, rows, cols, band_axis, row_axis),
        out_shape=[vmem(a.shape, F32) for a in results] + [vmem((2, 2, *half), F32)],
        in_specs=[anywhere] * 8,
        out_specs=[inside] * 6,
        scratch_shapes=[
            pltpu.SMEM(kernel_index.shape, jnp.int32),
            vmem((size, count, size), F32),
            vmem((2, 4, count, 128), F32),
            vmem(image.shape, F32),
            vmem(image.shape, F32),
            vmem((bands, 4 * rows, 384), BF16),
        ]
        + [vmem(line, F32)] * 4
        + [vmem(near, F32)] * 4
        + [vmem(far, F32)] * 4
        + [vmem((2, 2, *half), F32), vmem((2, *half), F32), vmem((2, *half), F32), vmem((2, 2, band_axis // 2, *half), F32)]
        + [dma((11,)), dma((1,)), dma((2,)), dma((2,))]
        + [dma((2, chunks))] * 4
        + [dma((2,))] * 2
        + [dma((2, band_axis // 2)), dma((2, 2, band_axis // 2))]
        + [dma((2,))] * 3
        + [pltpu.SemaphoreType.REGULAR],
        compiler_params=pltpu.CompilerParams(
            collective_id=0, has_side_effects=True, vmem_limit_bytes=24 * 1024 * 1024
        ),
    )(*[pltpu.with_memory_space_constraint(a, hbm) for a in inputs])
    return pl.pallas_call(
        finish_kernel,
        out_shape=[hbm(a.shape, F32) for a in results],
        in_specs=[inside] * 6,
        out_specs=[anywhere] * 5,
        scratch_shapes=[vmem(dual_sym.shape, F32), vmem(dual_grad.shape, F32), dma((3,)), dma((chunks,)), dma((chunks,))],
        compiler_params=pltpu.CompilerParams(vmem_limit_bytes=16 * 1024 * 1024),
    )(*[pltpu.with_memory_space_constraint(a, vmem) for a in held])


def solution(mesh):
    placed = (
        P("band", "row", None),
        P("band", "row", None),
        P(None, "band", "row", None),
        P(None, "band", "row", None),
        P(None, "band", "row", None),
        P("band", "row", None),
        P(),
        P("band"),
    )
    return jax.shard_map(
        functools.partial(body, mesh.shape["band"], mesh.shape["row"]),
        mesh=mesh,
        in_specs=placed,
        out_specs=(
            P("band", "row", None),
            P(None, "band", "row", None),
            P(None, "band", "row", None),
            P(None, "band", "row", None),
            P("band", "row", None),
        ),
        check_vma=False,
    )
```
